32 devices in a mesh: dp: 2 (over x), seq: 16 (over z, y, core).
Axes of the slice: x: 2, y: 2, z: 4, core: 2. Of those that a mesh axis runs over, the one named last changes fastest.
Arguments:
- spatial_qkv: bfloat16 [3, 4096, 1536], P(None, ('dp', 'seq')), parts along dimension 1, may hold values from -6 to 6
- temporal_qkv: bfloat16 [3, 4096, 1536], P(None, ('dp', 'seq')), parts along dimension 1, may hold values from -6 to 6
- cross_query: bfloat16 [4096, 1536], P(('dp', 'seq')), parts along dimension 0, may hold values from -6 to 6
- caption_kv: bfloat16 [640, 2, 1536], P(('dp', 'seq')), parts along dimension 0, may hold values from -6 to 6
- out_grad: bfloat16 [4096, 1536], P(('dp', 'seq')), parts along dimension 0, may hold values from -6 to 6
- live_tokens: int32 [2], P('dp'), parts along dimension 0, may hold values from 512 to 2048, as said below
- caption_len: int32 [2], P('dp'), parts along dimension 0, may hold values from 80 to 320, as said below
Outputs:
- mixed: bfloat16 [4096, 1536], P(('dp', 'seq')), parts along dimension 0
- spatial_grads: bfloat16 [3, 4096, 1536], P(None, ('dp', 'seq')), parts along dimension 1
- temporal_grads: bfloat16 [3, 4096, 1536], P(None, ('dp', 'seq')), parts along dimension 1
- cross_query_grad: bfloat16 [4096, 1536], P(('dp', 'seq')), parts along dimension 0
- caption_grads: float32 [640, 2, 1536], P(('dp', 'seq')), parts along dimension 0
The draws below stay inside these ranges and needn't reach their ends.
There are 2 independent parts, one for each index of `dp`. The reference program is written for one: setup_inputs(seed, part) draws one part's arguments, and reference() takes and returns one part's arrays. A program takes and returns all parts, laid end to end along the dimension named above; each array names one. Nothing has to cross between parts.
Inputs may be any that keep to these rules, and one draw needn't show every extreme that they name: Tokens from live_tokens on are padding. Caption rows from caption_len on are padding.
All inputs are finite; a program needn't handle non-finite values.
Results may differ from the reference program's by a relative error of at most 0.035.
Values may be sent and summed in bfloat16 or wider, within the bound.
A program may use at most 128 MiB of HBM per device.

```python
import jax
import jax.numpy as jnp
from jax import lax

HEADS = 12
HDIM = 128
P_SIZE = 512
CAPMAX = 320
HW = 1536
TOKENS = 2048


def draw_spatial_qkv(key, part):
    key = jax.random.fold_in(key, 3)
    key_one = jax.random.fold_in(key, 0)
    full_shape = (3, TOKENS, HEADS * HDIM)
    return jnp.clip(jax.random.normal(key_one, full_shape, jnp.float32), -6.0, 6.0).astype(jnp.bfloat16)


def draw_temporal_qkv(key, part):
    key = jax.random.fold_in(key, 5)
    key_one = jax.random.fold_in(key, 0)
    full_shape = (3, TOKENS, HEADS * HDIM)
    return jnp.clip(jax.random.normal(key_one, full_shape, jnp.float32), -6.0, 6.0).astype(jnp.bfloat16)


def draw_cross_query(key, part):
    key = jax.random.fold_in(key, 7)
    full_shape = (TOKENS, HEADS * HDIM)
    return jnp.clip(jax.random.normal(key, full_shape, jnp.float32), -6.0, 6.0).astype(jnp.bfloat16)


def draw_caption_kv(key, part):
    key = jax.random.fold_in(key, 8)
    key_one = jax.random.fold_in(key, 0)
    full_shape = (CAPMAX, 2, HEADS * HDIM)
    return jnp.clip(jax.random.normal(key_one, full_shape, jnp.float32), -6.0, 6.0).astype(jnp.bfloat16)


def draw_live_tokens(key, part):
    key = jax.random.fold_in(key, 9)
    drawn = jax.random.randint(key, (1,), TOKENS // 4, TOKENS + 1)
    return jnp.where(part == 1, TOKENS, drawn).astype(jnp.int32)


def draw_caption_len(key, part):
    key = jax.random.fold_in(key, 10)
    drawn = jax.random.randint(key, (1,), CAPMAX // 4, CAPMAX + 1)
    return jnp.where(part == 1, CAPMAX, drawn).astype(jnp.int32)


def block_scale(own_key, dims, cuts, smallest, high):
    level, own = 1.0, jax.random.fold_in(own_key, 6)
    for dim, shards_of in cuts:
        steps = jnp.exp(jax.random.uniform(jax.random.fold_in(own, dim), (shards_of,), jnp.float32, smallest / len(cuts), high / len(cuts)))
        level = level * jnp.repeat(steps, dims[dim] // shards_of).reshape([-1 if axis == dim else 1 for axis in range(len(dims))])
    return level


def scatter_about(key, extent, width, reach, cuts=(), kind=jnp.bfloat16):
    values = jax.random.normal(key, extent, jnp.float32) * width
    if len(cuts) > 0:
        values = block_scale(key, extent, cuts, -0.22, 0.18) * values
    return jnp.clip(values, min=-reach, max=reach).astype(kind)


def setup_inputs(seed: int = 0, part: int = 0) -> dict:
    seeds = jax.random.split(jax.random.key(seed), 8)
    part_keys = jax.random.split(jax.random.fold_in(seeds[7], part), 8)
    spatial_qkv = draw_spatial_qkv(jax.random.fold_in(jax.random.fold_in(seeds[7], part), 71), part)
    temporal_qkv = draw_temporal_qkv(jax.random.fold_in(jax.random.fold_in(seeds[7], part), 71), part)
    cross_query = draw_cross_query(jax.random.fold_in(jax.random.fold_in(seeds[7], part), 71), part)
    caption_kv = draw_caption_kv(jax.random.fold_in(jax.random.fold_in(seeds[7], part), 71), part)
    out_grad = scatter_about(part_keys[4], (TOKENS, HW), 1.0, 6.0, ((0, 16),))
    live_tokens = draw_live_tokens(jax.random.fold_in(jax.random.fold_in(seeds[7], part), 71), part)
    caption_len = draw_caption_len(jax.random.fold_in(jax.random.fold_in(seeds[7], part), 71), part)
    return {"spatial_qkv": spatial_qkv, "temporal_qkv": temporal_qkv, "cross_query": cross_query, "caption_kv": caption_kv, "out_grad": out_grad, "live_tokens": live_tokens, "caption_len": caption_len}


def attention_core(queries, key_rows, value_rows, grad_rows, key_keep):
    scale_factor = HDIM ** -0.5
    query_float = queries.astype(jnp.float32)
    key_float = key_rows.astype(jnp.float32)
    value_float = value_rows.astype(jnp.float32)
    grad_float = grad_rows.astype(jnp.float32)
    scores = jnp.einsum('bnhe,bmhe->bhnm', query_float, key_float) * scale_factor
    scores = jnp.where(key_keep, scores, -1e30)
    largest = jnp.max(scores, axis=-1)
    denominator = jnp.sum(jnp.exp(scores - largest[..., None]), axis=-1)
    weights = jnp.exp(scores - largest[..., None]) / denominator[..., None]
    weights_low = weights.astype(jnp.bfloat16)
    branch = jnp.einsum('bhnm,bmhe->bnhe', weights_low.astype(jnp.float32), value_float).astype(jnp.bfloat16)
    row_delta = jnp.einsum('bnhe,bnhe->bhn', grad_float, branch.astype(jnp.float32))
    dprobs = jnp.einsum('bnhe,bmhe->bhnm', grad_float, value_float)
    dscores = (weights * (dprobs - row_delta[..., None])).astype(jnp.bfloat16)
    slope_float = dscores.astype(jnp.float32)
    query_grad = jnp.einsum('bhnm,bmhe->bnhe', slope_float, key_float) * scale_factor
    key_grad = jnp.einsum('bhnm,bnhe->bmhe', slope_float, query_float) * scale_factor
    value_grad = jnp.einsum('bhnm,bnhe->bmhe', weights_low.astype(jnp.float32), grad_float)
    return branch, query_grad, key_grad, value_grad


def reference(spatial_qkv, temporal_qkv, cross_query, caption_kv, out_grad, live_tokens, caption_len):
    frames = TOKENS // P_SIZE
    feature_width = HEADS * HDIM
    token_ids = jnp.arange(TOKENS)
    live_rows = token_ids < live_tokens[0]
    grad_rows = jnp.where(live_rows[:, None], out_grad, jnp.zeros_like(out_grad))

    def framed(tensor):
        return tensor.reshape(frames, P_SIZE, HEADS, HDIM)

    def flatten(tensor):
        return tensor.reshape(TOKENS, feature_width)

    every_key = jnp.ones((P_SIZE,), jnp.bool_)

    def spatial_frame(pieces):
        results = attention_core(pieces[0][None], pieces[1][None], pieces[2][None], pieces[3][None], every_key)
        return tuple(item[0] for item in results)

    spatial = lax.map(spatial_frame, (framed(spatial_qkv[0]), framed(spatial_qkv[1]), framed(spatial_qkv[2]), framed(grad_rows)))

    def by_pixel(tensor):
        return jnp.swapaxes(framed(tensor), 0, 1)

    pixel_ids = jnp.arange(P_SIZE)
    frame_ids = jnp.arange(frames)
    frame_keep = (frame_ids[None, :] * P_SIZE + pixel_ids[:, None]) < live_tokens[0]
    frame_keep = frame_keep.reshape(P_SIZE, 1, 1, frames)
    temporal = attention_core(by_pixel(temporal_qkv[0]), by_pixel(temporal_qkv[1]), by_pixel(temporal_qkv[2]), by_pixel(grad_rows), frame_keep)
    temporal = tuple(jnp.swapaxes(item, 0, 1) for item in temporal)

    caption_keys = caption_kv[:, 0].reshape(1, CAPMAX, HEADS, HDIM)
    caption_values = caption_kv[:, 1].reshape(1, CAPMAX, HEADS, HDIM)
    caption_keep = jnp.arange(CAPMAX) < caption_len[0]

    def cross_frame(carry, pieces):
        results = attention_core(pieces[0][None], caption_keys, caption_values, pieces[1][None], caption_keep)
        return (carry[0] + results[2][0], carry[1] + results[3][0]), (results[0][0], results[1][0])

    zero_grad = jnp.zeros((CAPMAX, HEADS, HDIM), jnp.float32)
    sums_out, rows_out = lax.scan(cross_frame, (zero_grad, zero_grad), (framed(cross_query), framed(grad_rows)))
    total_rows = flatten(spatial[0]).astype(jnp.float32) + flatten(temporal[0]).astype(jnp.float32) + flatten(rows_out[0]).astype(jnp.float32)
    mixed = jnp.where(live_rows[:, None], total_rows, 0.0).astype(jnp.bfloat16)
    spatial_grads = jnp.stack([flatten(spatial[1]), flatten(spatial[2]), flatten(spatial[3])]).astype(jnp.bfloat16)
    temporal_grads = jnp.stack([flatten(temporal[1]), flatten(temporal[2]), flatten(temporal[3])]).astype(jnp.bfloat16)
    cross_query_grad = flatten(rows_out[1]).astype(jnp.bfloat16)
    caption_grads = jnp.stack([sums_out[0].reshape(CAPMAX, feature_width), sums_out[1].reshape(CAPMAX, feature_width)], axis=1)
    return (mixed, spatial_grads, temporal_grads, cross_query_grad, caption_grads)
```

```python
import functools

import jax
import jax.numpy as jnp
from jax import lax
from jax.experimental import pallas as pl
from jax.experimental.pallas import tpu as pltpu
from jax.sharding import PartitionSpec as P

HDIM = 128
P_SIZE = 512
F32 = jnp.float32
BF16 = jnp.bfloat16
LOW = -1e30


def dot_nt(a, b):
    return lax.dot_general(a, b, (((1,), (1,)), ((), ())), preferred_element_type=F32)


def dot_tn(a, b):
    return lax.dot_general(a, b, (((0,), (0,)), ((), ())), preferred_element_type=F32)


def dot_nn(a, b):
    return lax.dot_general(a, b, (((1,), (0,)), ((), ())), preferred_element_type=F32)


def flat(x):
    rows = 1
    for n in x.shape[:-1]:
        rows *= n
    if x.shape[-2] % 16:
        return x.astype(F32).reshape(rows, x.shape[-1]).astype(BF16)
    return x.reshape(rows, x.shape[-1])


def unflat(x, shape):
    if shape[-2] % 16:
        return x.reshape(shape).astype(BF16)
    return x.astype(BF16).reshape(shape)


def slopes(q, k, v, g, scale, bias):
    s = dot_nt(k, q) * scale
    if bias is not None:
        s = s + bias
    p = jnp.exp(s - jnp.max(s, axis=0, keepdims=True))
    w = p * (1.0 / jnp.sum(p, axis=0, keepdims=True))
    dp = dot_nt(v, g)
    delta = jnp.sum(w * dp, axis=0, keepdims=True)
    return w.astype(BF16), (w * (dp - delta)).astype(BF16)


def kernel(
    geo,
    live_ref, clen_ref, sqkv, tqkv, cq, cap, og,
    mixed, sgrad, tgrad, cqgrad, capgrad,
    srecv, sres, trecv, tres, crecv, cf, ckv, cbias, cacc, cg, cgr, fin, spo, tmo, wbuf, dbuf,
    loc, t_s, t_r, tb_s, tb_r, s_s, s_r, sb_s, sb_r, c1_s, c1_r, c2_s, c2_r, c3_s, c3_r, c4_s, c4_r,
):
    G, F, pix, W, HC, R, RP = geo
    S = G * F
    KP = S * RP
    T = F * pix
    scale = HDIM ** (-0.5)
    dev = lax.axis_index("seq")
    f = dev // G
    g = dev % G
    live = live_ref[0]
    clen = clen_ref[0]

    def cols(i):
        return pl.ds(pl.multiple_of(i * W, 128), W)

    def hcols(h):
        return pl.ds(pl.multiple_of(h * HDIM, 128), HDIM)

    def mate(o):
        return (g + o) % G

    def mate_from(o):
        return (g + G - o) % G

    def line(o):
        return (f + o) % F

    def line_from(o):
        return (f + F - o) % F

    def at_mate(i):
        return f * G + i

    def at_line(i):
        return i * G + g

    def remote(src, dst, ss, rs, to):
        return pltpu.make_async_remote_copy(
            src_ref=src, dst_ref=dst, send_sem=ss, recv_sem=rs,
            device_id={"seq": to}, device_id_type=pl.DeviceIdType.MESH,
        )

    barrier = pltpu.get_barrier_semaphore()
    for o in range(1, G):
        pl.semaphore_signal(barrier, inc=1, device_id={"seq": at_mate(mate(o))}, device_id_type=pl.DeviceIdType.MESH)
    for o in range(1, F):
        pl.semaphore_signal(barrier, inc=1, device_id={"seq": at_line(line(o))}, device_id_type=pl.DeviceIdType.MESH)

    local = [
        pltpu.make_async_copy(cap.at[:, :, cols(g)], crecv.at[dev], loc.at[0]),
        pltpu.make_async_copy(sqkv.at[:, :, :, cols(g)], srecv.at[pl.ds(0, 3), g], loc.at[1]),
        pltpu.make_async_copy(og.at[:, :, cols(g)], srecv.at[3, g], loc.at[2]),
        pltpu.make_async_copy(cq.at[:, :, cols(g)], srecv.at[4, g], loc.at[3]),
    ]
    for c in range(G):
        local.append(pltpu.make_async_copy(tqkv.at[:, f, :, cols(c)], trecv.at[c, pl.ds(0, 3), f], loc.at[4 + 2 * c]))
        local.append(pltpu.make_async_copy(og.at[f, :, cols(c)], trecv.at[c, 3, f], loc.at[5 + 2 * c]))
    for copy in local:
        copy.start()
    pl.semaphore_wait(barrier, G + F - 2)

    def c1(o):
        return remote(cap.at[:, :, cols(mate(o))], crecv.at[dev], c1_s.at[o], c1_r.at[o], at_mate(mate(o)))

    def c1_in(o):
        i = mate_from(o)
        return remote(cap.at[:, :, cols(i)], crecv.at[at_mate(i)], c1_s.at[o], c1_r.at[o], at_mate(i))

    def t_out(c, o):
        j = line(o)
        return (
            remote(tqkv.at[:, j, :, cols(c)], trecv.at[c, pl.ds(0, 3), f], t_s.at[c, o, 0], t_r.at[c, o, 0], at_line(j)),
            remote(og.at[j, :, cols(c)], trecv.at[c, 3, f], t_s.at[c, o, 1], t_r.at[c, o, 1], at_line(j)),
        )

    def t_in(c, o):
        j = line_from(o)
        return (
            remote(tqkv.at[:, j, :, cols(c)], trecv.at[c, pl.ds(0, 3), j], t_s.at[c, o, 0], t_r.at[c, o, 0], at_line(j)),
            remote(og.at[j, :, cols(c)], trecv.at[c, 3, j], t_s.at[c, o, 1], t_r.at[c, o, 1], at_line(j)),
        )

    def s_out(o):
        i = mate(o)
        return (
            remote(sqkv.at[:, :, :, cols(i)], srecv.at[pl.ds(0, 3), g], s_s.at[o, 0], s_r.at[o, 0], at_mate(i)),
            remote(og.at[:, :, cols(i)], srecv.at[3, g], s_s.at[o, 1], s_r.at[o, 1], at_mate(i)),
            remote(cq.at[:, :, cols(i)], srecv.at[4, g], s_s.at[o, 2], s_r.at[o, 2], at_mate(i)),
        )

    def s_in(o):
        i = mate_from(o)
        return (
            remote(sqkv.at[:, :, :, cols(i)], srecv.at[pl.ds(0, 3), i], s_s.at[o, 0], s_r.at[o, 0], at_mate(i)),
            remote(og.at[:, :, cols(i)], srecv.at[3, i], s_s.at[o, 1], s_r.at[o, 1], at_mate(i)),
            remote(cq.at[:, :, cols(i)], srecv.at[4, i], s_s.at[o, 2], s_r.at[o, 2], at_mate(i)),
        )

    for o in range(1, G):
        c1(o).start()
    for o in range(1, F):
        for copy in t_out(0, o):
            copy.start()
    for o in range(1, G):
        for copy in s_out(o):
            copy.start()
    for c in range(1, G):
        for o in range(1, F):
            for copy in t_out(c, o):
                copy.start()

    def c2(o):
        rows = pl.ds(f * G, G)
        return remote(crecv.at[rows], crecv.at[rows], c2_s.at[o], c2_r.at[o], at_line(line(o)))

    def c2_in(o):
        rows = pl.ds(line_from(o) * G, G)
        return remote(crecv.at[rows], crecv.at[rows], c2_s.at[o], c2_r.at[o], at_line(line_from(o)))

    local[0].wait()
    for o in range(1, G):
        c1_in(o).wait_recv()
    for o in range(1, F):
        c2(o).start()

    cf[...] = jnp.zeros(cf.shape, F32)
    cbias[...] = jnp.full(cbias.shape, LOW, F32)

    def live_rows(x, first):
        ids = first + lax.broadcasted_iota(jnp.int32, x.shape, 0)
        return jnp.where(ids < live, x.astype(F32), 0.0).astype(BF16)

    def many(k, v, q, gr, keys, bias):
        for b in range(G):
            rows = slice(b * T, (b + 1) * T)
            w, d = slopes(q[rows], k, v, gr[rows], scale, bias)
            wbuf[pl.ds(0, keys), rows] = w
            dbuf[pl.ds(0, keys), rows] = d
        w = wbuf[pl.ds(0, keys), :]
        d = dbuf[pl.ds(0, keys), :]
        return dot_tn(w, v), dot_tn(d, k) * scale, dot_nn(d, q) * scale, dot_nn(w, gr)

    for copy in local[1:4]:
        copy.wait()
    for o in range(1, G):
        for copy in s_in(o):
            copy.wait_recv()

    block = (G, F, pix, HDIM)

    @pl.loop(0, HC)
    def _(h):
        at = hcols(h)
        q, k, v = (flat(srecv[i, :, :, :, at]) for i in range(3))
        gr = live_rows(flat(srecv[3, :, :, :, at]), f * (G * T))
        out, dq, dk, dv = many(k, v, q, gr, G * T, None)
        sres[0, :, :, :, at] = unflat(out, block)
        sres[1, :, :, :, at] = unflat(dq, block)
        sres[2, :, :, :, at] = unflat(dk, block)
        sres[3, :, :, :, at] = unflat(dv, block)

    def sb_grads(o, i, src_i):
        return remote(sres.at[pl.ds(1, 3), i], sgrad.at[:, :, :, cols(src_i)], sb_s.at[o, 0], sb_r.at[o, 0], at_mate(i))

    def sb_cross(o, i, src_i):
        return (
            remote(sres.at[0, i], spo.at[:, :, cols(src_i)], sb_s.at[o, 1], sb_r.at[o, 1], at_mate(i)),
            remote(sres.at[4, i], cqgrad.at[:, :, cols(src_i)], sb_s.at[o, 2], sb_r.at[o, 2], at_mate(i)),
        )

    for o in range(1, G):
        sb_grads(o, mate(o), g).start()
    home = [pltpu.make_async_copy(sres.at[pl.ds(1, 3), g], sgrad.at[:, :, :, cols(g)], loc.at[0])]
    home[0].start()

    rk = lax.broadcasted_iota(jnp.int32, (T, T), 0)
    rq = lax.broadcasted_iota(jnp.int32, (T, T), 1)
    shift = pix.bit_length() - 1
    first = g * T + f * pix
    key_token = (rk >> shift) * P_SIZE + (rk & (pix - 1)) + first
    same = ((rk & (pix - 1)) == (rq & (pix - 1))) & (key_token < live)
    tbias = jnp.where(same, 0.0, LOW)
    rd = lax.broadcasted_iota(jnp.int32, (T, HDIM), 0)
    t_live = ((rd >> shift) * P_SIZE + (rd & (pix - 1)) + first) < live

    def tb(c, o, j, src_j):
        return (
            remote(tres.at[c, 0, j], tmo.at[src_j, :, cols(c)], tb_s.at[c, o, 0], tb_r.at[c, o, 0], at_line(j)),
            remote(tres.at[c, pl.ds(1, 3), j], tgrad.at[:, src_j, :, cols(c)], tb_s.at[c, o, 1], tb_r.at[c, o, 1], at_line(j)),
        )

    tblock = (F, pix, HDIM)

    for c in range(G):
        local[4 + 2 * c].wait()
        local[5 + 2 * c].wait()

    @pl.loop(0, G)
    def _(c):
        for o in range(1, F):
            for copy in t_in(c, o):
                copy.wait_recv()
        for h in range(HC):
            at = pl.ds(h * HDIM, HDIM)
            q, k, v, gr = (flat(trecv[c, i, :, :, at]) for i in range(4))
            gr = jnp.where(t_live, gr.astype(F32), 0.0).astype(BF16)
            w, d = slopes(q, k, v, gr, scale, tbias)
            tres[c, 0, :, :, at] = unflat(dot_tn(w, v), tblock)
            tres[c, 1, :, :, at] = unflat(dot_tn(d, k) * scale, tblock)
            tres[c, 2, :, :, at] = unflat(dot_nn(d, q) * scale, tblock)
            tres[c, 3, :, :, at] = unflat(dot_nn(w, gr), tblock)
        for o in range(1, F):
            for copy in tb(c, o, line(o), f):
                copy.start()

    for c in range(G):
        home.append(pltpu.make_async_copy(tres.at[c, 0, f], tmo.at[f, :, cols(c)], loc.at[4 + 2 * c]))
        home.append(pltpu.make_async_copy(tres.at[c, pl.ds(1, 3), f], tgrad.at[:, f, :, cols(c)], loc.at[5 + 2 * c]))
    for copy in home[1:]:
        copy.start()

    for o in range(1, F):
        c2_in(o).wait_recv()

    @pl.loop(0, S)
    def _(s):
        at = pl.ds(pl.multiple_of(s * RP, 8), R)
        for i in range(2):
            cf[i, at, :] = crecv[s, i].astype(F32)
        ids = s * R + lax.broadcasted_iota(jnp.int32, (R, HDIM), 0)
        cbias[at, :] = jnp.where(ids < clen, 0.0, LOW)

    ckv[...] = cf[...].astype(BF16)

    @pl.loop(0, HC)
    def _(h):
        at = hcols(h)
        q = flat(srecv[4, :, :, :, at])
        gr = live_rows(flat(srecv[3, :, :, :, at]), f * (G * T))
        k = ckv[0, :, at]
        v = ckv[1, :, at]
        out, dq, dk, dv = many(k, v, q, gr, KP, cbias[...])
        total = flat(sres[0, :, :, :, at]).astype(F32) + out
        sres[0, :, :, :, at] = unflat(total, block)
        sres[4, :, :, :, at] = unflat(dq, block)
        cacc[0, :, at] = dk
        cacc[1, :, at] = dv

    @pl.loop(0, S)
    def _(s):
        at = pl.ds(pl.multiple_of(s * RP, 8), R)
        for i in range(2):
            cg[s, i] = cacc[i, at, :].astype(BF16)

    def c3(o):
        j = line(o)
        return remote(cg.at[pl.ds(j * G, G)], cgr.at[f], c3_s.at[o], c3_r.at[o], at_line(j))

    def c3_in(o):
        j = line_from(o)
        return remote(cg.at[pl.ds(j * G, G)], cgr.at[j], c3_s.at[o], c3_r.at[o], at_line(j))

    for o in range(1, F):
        c3(o).start()
    for o in range(1, G):
        for copy in sb_cross(o, mate(o), g):
            copy.start()
    home.append(pltpu.make_async_copy(sres.at[0, g], spo.at[:, :, cols(g)], loc.at[1]))
    home.append(pltpu.make_async_copy(sres.at[4, g], cqgrad.at[:, :, cols(g)], loc.at[2]))
    home[-2].start()
    home[-1].start()

    for o in range(1, F):
        c3_in(o).wait_recv()
    for i in range(G):
        at = pl.ds(pl.multiple_of((f * G + i) * RP, 8), R)
        for b in range(2):
            total = cacc[b, at, :]
            for o in range(1, F):
                total = total + cgr[line_from(o), i, b].astype(F32)
            fin[i, b] = total

    def c4(o, i, src_i):
        return remote(fin.at[i], capgrad.at[:, :, cols(src_i)], c4_s.at[o], c4_r.at[o], at_mate(i))

    for o in range(1, G):
        c4(o, mate(o), g).start()
    home.append(pltpu.make_async_copy(fin.at[g], capgrad.at[:, :, cols(g)], loc.at[3]))
    home[-1].start()

    for o in range(1, G):
        i = mate_from(o)
        sb_grads(o, i, i).wait_recv()
        for copy in sb_cross(o, i, i):
            copy.wait_recv()
    for copy in home:
        copy.wait()

    @pl.loop(0, G)
    def _(c):
        for o in range(1, F):
            j = line_from(o)
            for copy in tb(c, o, j, j):
                copy.wait_recv()

    shape3 = (F, pix, W)
    tok = (
        dev * T
        + lax.broadcasted_iota(jnp.int32, shape3, 0) * pix
        + lax.broadcasted_iota(jnp.int32, shape3, 1)
    )
    for c in range(G):
        at = slice(c * W, (c + 1) * W)
        total = spo[:, :, at].astype(F32) + tmo[:, :, at].astype(F32)
        mixed[:, :, at] = jnp.where(tok < live, total, 0.0).astype(BF16)

    for o in range(1, G):
        i = mate_from(o)
        c4(o, i, i).wait_recv()

    for o in range(1, G):
        c1(o).wait_send()
        for copy in s_out(o):
            copy.wait_send()
        sb_grads(o, mate(o), g).wait_send()
        for copy in sb_cross(o, mate(o), g):
            copy.wait_send()
        c4(o, mate(o), g).wait_send()
    for o in range(1, F):
        c2(o).wait_send()
        c3(o).wait_send()

    @pl.loop(0, G)
    def _(c):
        for o in range(1, F):
            for copy in t_out(c, o):
                copy.wait_send()
            for copy in tb(c, o, line(o), f):
                copy.wait_send()


def local(spatial_qkv, temporal_qkv, cross_query, caption_kv, out_grad, live_tokens, caption_len):
    devices = lax.axis_size("seq")
    rows, width = out_grad.shape
    G = P_SIZE // rows
    F = devices // G
    pix = rows // F
    W = width // G
    HC = W // HDIM
    R = caption_kv.shape[0]
    RP = (R + 7) // 8 * 8
    S = G * F
    KP = S * RP
    keys = max(KP, G * rows)
    geo = (G, F, pix, W, HC, R, RP)
    dma = pltpu.SemaphoreType.DMA
    any_spec = pl.BlockSpec(memory_space=pl.ANY)
    smem = pl.BlockSpec(memory_space=pltpu.SMEM)
    vmem = pl.BlockSpec(memory_space=pltpu.VMEM)
    mixed, sgrad, tgrad, cqgrad, capgrad = pl.pallas_call(
        functools.partial(kernel, geo),
        out_shape=(
            jax.ShapeDtypeStruct((F, pix, width), BF16),
            jax.ShapeDtypeStruct((3, F, pix, width), BF16),
            jax.ShapeDtypeStruct((3, F, pix, width), BF16),
            jax.ShapeDtypeStruct((F, pix, width), BF16),
            jax.ShapeDtypeStruct((2, R, width), F32),
        ),
        in_specs=[smem, smem] + [any_spec] * 5,
        out_specs=(vmem, any_spec, any_spec, any_spec, any_spec),
        scratch_shapes=[
            pltpu.VMEM((5, G, F, pix, W), BF16),
            pltpu.VMEM((5, G, F, pix, W), BF16),
            pltpu.VMEM((G, 4, F, pix, W), BF16),
            pltpu.VMEM((G, 4, F, pix, W), BF16),
            pltpu.VMEM((S, 2, R, W), BF16),
            pltpu.VMEM((2, KP, W), F32),
            pltpu.VMEM((2, KP, W), BF16),
            pltpu.VMEM((KP, HDIM), F32),
            pltpu.VMEM((2, KP, W), F32),
            pltpu.VMEM((S, 2, R, W), BF16),
            pltpu.VMEM((F, G, 2, R, W), BF16),
            pltpu.VMEM((G, 2, R, W), F32),
            pltpu.VMEM((F, pix, width), BF16),
            pltpu.VMEM((F, pix, width), BF16),
            pltpu.VMEM((keys, G * rows), BF16),
            pltpu.VMEM((keys, G * rows), BF16),
            dma((4 + 2 * G,)),
            dma((G, F, 2)), dma((G, F, 2)),
            dma((G, F, 2)), dma((G, F, 2)),
            dma((G, 3)), dma((G, 3)),
            dma((G, 3)), dma((G, 3)),
            dma((G,)), dma((G,)),
            dma((F,)), dma((F,)),
            dma((F,)), dma((F,)),
            dma((G,)), dma((G,)),
        ],
        compiler_params=pltpu.CompilerParams(
            collective_id=0, has_side_effects=True, vmem_limit_bytes=48 * 1024 * 1024
        ),
    )(
        live_tokens,
        caption_len,
        spatial_qkv.reshape(3, F, pix, width),
        temporal_qkv.reshape(3, F, pix, width),
        cross_query.reshape(F, pix, width),
        jnp.swapaxes(caption_kv, 0, 1),
        out_grad.reshape(F, pix, width),
    )
    return (
        mixed.reshape(rows, width),
        sgrad.reshape(3, rows, width),
        tgrad.reshape(3, rows, width),
        cqgrad.reshape(rows, width),
        jnp.swapaxes(capgrad, 0, 1),
    )


def solution(mesh):
    placed = (
        P(None, ("dp", "seq"), None),
        P(None, ("dp", "seq"), None),
        P(("dp", "seq"), None),
        P(("dp", "seq"), None, None),
        P(("dp", "seq"), None),
        P("dp"),
        P("dp"),
    )
    return jax.shard_map(
        local,
        mesh=mesh,
        in_specs=placed,
        out_specs=(
            P(("dp", "seq"), None),
            P(None, ("dp", "seq"), None),
            P(None, ("dp", "seq"), None),
            P(("dp", "seq"), None),
            P(("dp", "seq"), None, None),
        ),
        check_vma=False,
    )
```

```python
import functools

import jax
import jax.numpy as jnp
from jax import lax
from jax.experimental import pallas as pl
from jax.experimental.pallas import tpu as pltpu
from jax.sharding import PartitionSpec as P

HDIM = 128
P_SIZE = 512
F32 = jnp.float32
BF16 = jnp.bfloat16
LOW = -1e30


def dot_nt(a, b):
    return lax.dot_general(a, b, (((1,), (1,)), ((), ())), preferred_element_type=F32)


def dot_tn(a, b):
    return lax.dot_general(a, b, (((0,), (0,)), ((), ())), preferred_element_type=F32)


def dot_nn(a, b):
    return lax.dot_general(a, b, (((1,), (0,)), ((), ())), preferred_element_type=F32)


def flat(x):
    rows = 1
    for n in x.shape[:-1]:
        rows *= n
    if x.shape[-2] % 16:
        return x.astype(F32).reshape(rows, x.shape[-1]).astype(BF16)
    return x.reshape(rows, x.shape[-1])


def unflat(x, shape):
    if shape[-2] % 16:
        return x.reshape(shape).astype(BF16)
    return x.astype(BF16).reshape(shape)


def slopes(q, k, v, g, scale, bias):
    s = dot_nt(k, q) * scale
    if bias is not None:
        s = s + bias
    p = jnp.exp(s - jnp.max(s, axis=0, keepdims=True))
    w = p * (1.0 / jnp.sum(p, axis=0, keepdims=True))
    dp = dot_nt(v, g)
    delta = jnp.sum(w * dp, axis=0, keepdims=True)
    return w.astype(BF16), (w * (dp - delta)).astype(BF16)


def kernel(
    geo,
    live_ref, clen_ref, sqkv, tqkv, cq, cap, og,
    mixed, sgrad, tgrad, cqgrad, capgrad,
    srecv, sres, trecv, tres, crecv, cf, ckv, cbias, cacc, cg, cgu, cgd, fin, spo, tmo, wbuf, dbuf, tbias,
    loc, t_s, t_r, tb_s, tb_r, s_s, s_r, sb_s, sb_r, c1_s, c1_r, c2_s, c2_r, c3_s, c3_r, c4_s, c4_r,
):
    G, F, pix, W, HC, R, RP = geo
    S = G * F
    KP = S * RP
    T = F * pix
    scale = HDIM ** (-0.5)
    dev = lax.axis_index("seq")
    f = dev // G
    g = dev % G
    live = live_ref[0]
    clen = clen_ref[0]

    def cols(i):
        return pl.ds(pl.multiple_of(i * W, 128), W)

    def hcols(h):
        return pl.ds(pl.multiple_of(h * HDIM, 128), HDIM)

    def mate(o):
        return (g + o) % G

    def mate_from(o):
        return (g + G - o) % G

    def line(o):
        return (f + o) % F

    def line_from(o):
        return (f + F - o) % F

    def at_mate(i):
        return f * G + i

    def at_line(i):
        return i * G + g

    def remote(src, dst, ss, rs, to):
        return pltpu.make_async_remote_copy(
            src_ref=src, dst_ref=dst, send_sem=ss, recv_sem=rs,
            device_id={"seq": to}, device_id_type=pl.DeviceIdType.MESH,
        )

    barrier = pltpu.get_barrier_semaphore()
    for o in range(1, G):
        pl.semaphore_signal(barrier, inc=1, device_id={"seq": at_mate(mate(o))}, device_id_type=pl.DeviceIdType.MESH)
    for o in range(1, F):
        pl.semaphore_signal(barrier, inc=1, device_id={"seq": at_line(line(o))}, device_id_type=pl.DeviceIdType.MESH)

    local = [
        pltpu.make_async_copy(cap.at[:, :, cols(g)], crecv.at[dev], loc.at[0]),
        pltpu.make_async_copy(sqkv.at[:, :, :, cols(g)], srecv.at[pl.ds(0, 3), g], loc.at[1]),
        pltpu.make_async_copy(og.at[:, :, cols(g)], srecv.at[3, g], loc.at[2]),
        pltpu.make_async_copy(cq.at[:, :, cols(g)], srecv.at[4, g], loc.at[3]),
    ]
    for c in range(G):
        local.append(pltpu.make_async_copy(tqkv.at[:, f, :, cols(c)], trecv.at[c, pl.ds(0, 3), f], loc.at[4 + 2 * c]))
        local.append(pltpu.make_async_copy(og.at[f, :, cols(c)], trecv.at[c, 3, f], loc.at[5 + 2 * c]))
    for copy in local:
        copy.start()
    pl.semaphore_wait(barrier, G + F - 2)

    def c1(o):
        return remote(cap.at[:, :, cols(mate(o))], crecv.at[dev], c1_s.at[o], c1_r.at[o], at_mate(mate(o)))

    def c1_in(o):
        i = mate_from(o)
        return remote(cap.at[:, :, cols(i)], crecv.at[at_mate(i)], c1_s.at[o], c1_r.at[o], at_mate(i))

    def t_out(c, o):
        j = line(o)
        return (
            remote(tqkv.at[:, j, :, cols(c)], trecv.at[c, pl.ds(0, 3), f], t_s.at[c, o, 0], t_r.at[c, o, 0], at_line(j)),
            remote(og.at[j, :, cols(c)], trecv.at[c, 3, f], t_s.at[c, o, 1], t_r.at[c, o, 1], at_line(j)),
        )

    def t_in(c, o):
        j = line_from(o)
        return (
            remote(tqkv.at[:, j, :, cols(c)], trecv.at[c, pl.ds(0, 3), j], t_s.at[c, o, 0], t_r.at[c, o, 0], at_line(j)),
            remote(og.at[j, :, cols(c)], trecv.at[c, 3, j], t_s.at[c, o, 1], t_r.at[c, o, 1], at_line(j)),
        )

    def s_out(o):
        i = mate(o)
        return (
            remote(sqkv.at[:, :, :, cols(i)], srecv.at[pl.ds(0, 3), g], s_s.at[o, 0], s_r.at[o, 0], at_mate(i)),
            remote(og.at[:, :, cols(i)], srecv.at[3, g], s_s.at[o, 1], s_r.at[o, 1], at_mate(i)),
            remote(cq.at[:, :, cols(i)], srecv.at[4, g], s_s.at[o, 2], s_r.at[o, 2], at_mate(i)),
        )

    def s_in(o):
        i = mate_from(o)
        return (
            remote(sqkv.at[:, :, :, cols(i)], srecv.at[pl.ds(0, 3), i], s_s.at[o, 0], s_r.at[o, 0], at_mate(i)),
            remote(og.at[:, :, cols(i)], srecv.at[3, i], s_s.at[o, 1], s_r.at[o, 1], at_mate(i)),
            remote(cq.at[:, :, cols(i)], srecv.at[4, i], s_s.at[o, 2], s_r.at[o, 2], at_mate(i)),
        )

    def send_chunk(c):
        for o in range(1, F):
            for copy in t_out(c, o):
                copy.start()

    for o in range(1, G):
        c1(o).start()
    send_chunk(0)
    for o in range(1, G):
        for copy in s_out(o):
            copy.start()

    def piece(i):
        return pl.ds(i * G, G)

    def up(i):
        return remote(crecv.at[piece(i)], crecv.at[piece(i)], c2_s.at[0, i], c2_r.at[0, i], at_line(line(1)))

    def down(i):
        return remote(crecv.at[piece(i)], crecv.at[piece(i)], c2_s.at[1, i], c2_r.at[1, i], at_line(line_from(1)))

    def gather_step(t):
        @pl.when(f >= t)
        def _():
            if t > 0:
                up(f - t).wait_recv()

            @pl.when(f < F - 1)
            def _():
                up(f - t).start()

        @pl.when(f + t < F)
        def _():
            if t > 0:
                down(f + t).wait_recv()

            @pl.when(f > 0)
            def _():
                down(f + t).start()

    local[0].wait()
    for o in range(1, G):
        c1_in(o).wait_recv()
    gather_step(0)
    send_chunk(1)

    cf[...] = jnp.zeros(cf.shape, F32)
    cbias[...] = jnp.full(cbias.shape, LOW, F32)

    def live_rows(x, first):
        ids = first + lax.broadcasted_iota(jnp.int32, x.shape, 0)
        return jnp.where(ids < live, x.astype(F32), 0.0).astype(BF16)

    def many(k, v, q, gr, keys, bias):
        for b in range(G):
            rows = slice(b * T, (b + 1) * T)
            w, d = slopes(q[rows], k, v, gr[rows], scale, bias)
            wbuf[pl.ds(0, keys), rows] = w
            dbuf[pl.ds(0, keys), rows] = d
        w = wbuf[pl.ds(0, keys), :]
        d = dbuf[pl.ds(0, keys), :]
        return dot_tn(w, v), dot_tn(d, k) * scale, dot_nn(d, q) * scale, dot_nn(w, gr)

    rk = lax.broadcasted_iota(jnp.int32, (T, T), 0)
    rq = lax.broadcasted_iota(jnp.int32, (T, T), 1)
    shift = pix.bit_length() - 1
    first = g * T + f * pix
    key_token = (rk >> shift) * P_SIZE + (rk & (pix - 1)) + first
    same = ((rk & (pix - 1)) == (rq & (pix - 1))) & (key_token < live)
    tbias[...] = jnp.where(same, 0.0, LOW)

    def tb(c, o, j, src_j):
        return (
            remote(tres.at[c, 0, j], tmo.at[src_j, :, cols(c)], tb_s.at[c, o, 0], tb_r.at[c, o, 0], at_line(j)),
            remote(tres.at[c, pl.ds(1, 3), j], tgrad.at[:, src_j, :, cols(c)], tb_s.at[c, o, 1], tb_r.at[c, o, 1], at_line(j)),
        )

    tblock = (F, pix, HDIM)
    home = []

    def temporal_chunk(c):
        for o in range(1, F):
            for copy in t_in(c, o):
                copy.wait_recv()
        rd = lax.broadcasted_iota(jnp.int32, (T, HDIM), 0)
        t_live = ((rd >> shift) * P_SIZE + (rd & (pix - 1)) + first) < live
        for h in range(HC):
            at = pl.ds(h * HDIM, HDIM)
            q, k, v, gr = (flat(trecv[c, i, :, :, at]) for i in range(4))
            gr = jnp.where(t_live, gr.astype(F32), 0.0).astype(BF16)
            w, d = slopes(q, k, v, gr, scale, tbias[...])
            tres[c, 0, :, :, at] = unflat(dot_tn(w, v), tblock)
            tres[c, 1, :, :, at] = unflat(dot_tn(d, k) * scale, tblock)
            tres[c, 2, :, :, at] = unflat(dot_nn(d, q) * scale, tblock)
            tres[c, 3, :, :, at] = unflat(dot_nn(w, gr), tblock)
        for o in range(1, F):
            for copy in tb(c, o, line(o), f):
                copy.start()

    def temporal_home(c):
        mine = [
            pltpu.make_async_copy(tres.at[c, 0, f], tmo.at[f, :, cols(c)], loc.at[4 + 2 * c]),
            pltpu.make_async_copy(tres.at[c, pl.ds(1, 3), f], tgrad.at[:, f, :, cols(c)], loc.at[5 + 2 * c]),
        ]
        for copy in mine:
            copy.start()
        home.extend(mine)

    for c in range(G):
        local[4 + 2 * c].wait()
        local[5 + 2 * c].wait()
    for t in range(1, max(F - 1, 3)):
        if t <= 2:
            temporal_chunk(t - 1)
            temporal_home(t - 1)
        if t < F - 1:
            gather_step(t)
        if t + 1 < G:
            send_chunk(t + 1)
    for c in range(max(F - 1, 3) + 1, G):
        send_chunk(c)

    for copy in local[1:4]:
        copy.wait()
    for o in range(1, G):
        for copy in s_in(o):
            copy.wait_recv()

    block = (G, F, pix, HDIM)

    @pl.loop(0, HC)
    def _(h):
        at = hcols(h)
        q, k, v = (flat(srecv[i, :, :, :, at]) for i in range(3))
        gr = live_rows(flat(srecv[3, :, :, :, at]), f * (G * T))
        out, dq, dk, dv = many(k, v, q, gr, G * T, None)
        sres[0, :, :, :, at] = unflat(out, block)
        sres[1, :, :, :, at] = unflat(dq, block)
        sres[2, :, :, :, at] = unflat(dk, block)
        sres[3, :, :, :, at] = unflat(dv, block)

    def sb_grads(o, i, src_i):
        return remote(sres.at[pl.ds(1, 3), i], sgrad.at[:, :, :, cols(src_i)], sb_s.at[o, 0], sb_r.at[o, 0], at_mate(i))

    def sb_cross(o, i, src_i):
        return (
            remote(sres.at[0, i], spo.at[:, :, cols(src_i)], sb_s.at[o, 1], sb_r.at[o, 1], at_mate(i)),
            remote(sres.at[4, i], cqgrad.at[:, :, cols(src_i)], sb_s.at[o, 2], sb_r.at[o, 2], at_mate(i)),
        )

    for o in range(1, G):
        sb_grads(o, mate(o), g).start()
    home.append(pltpu.make_async_copy(sres.at[pl.ds(1, 3), g], sgrad.at[:, :, :, cols(g)], loc.at[0]))
    home[-1].start()

    @pl.when(f == F - 1)
    def _():
        up(0).wait_recv()

    @pl.when(f == 0)
    def _():
        down(F - 1).wait_recv()

    @pl.loop(0, S)
    def _(s):
        at = pl.ds(pl.multiple_of(s * RP, 8), R)
        for i in range(2):
            cf[i, at, :] = crecv[s, i].astype(F32)
        ids = s * R + lax.broadcasted_iota(jnp.int32, (R, HDIM), 0)
        cbias[at, :] = jnp.where(ids < clen, 0.0, LOW)

    ckv[...] = cf[...].astype(BF16)

    @pl.loop(0, HC)
    def _(h):
        at = hcols(h)
        q = flat(srecv[4, :, :, :, at])
        gr = live_rows(flat(srecv[3, :, :, :, at]), f * (G * T))
        k = ckv[0, :, at]
        v = ckv[1, :, at]
        out, dq, dk, dv = many(k, v, q, gr, KP, cbias[...])
        total = flat(sres[0, :, :, :, at]).astype(F32) + out
        sres[0, :, :, :, at] = unflat(total, block)
        sres[4, :, :, :, at] = unflat(dq, block)
        cacc[0, :, at] = dk
        cacc[1, :, at] = dv

    @pl.loop(0, S)
    def _(s):
        at = pl.ds(pl.multiple_of(s * RP, 8), R)
        for i in range(2):
            cg[s, i] = cacc[i, at, :].astype(BF16)

    def c3_up(j):
        return remote(cg.at[piece(j)], cgu.at[j], c3_s.at[0, j], c3_r.at[0, j], at_line(line(1)))

    def c3_down(j):
        return remote(cg.at[piece(j)], cgd.at[j], c3_s.at[1, j], c3_r.at[1, j], at_line(line_from(1)))

    def reduce_step(t):
        def hop(j, send, arrived):
            if t > 0:
                send.wait_recv()
                cg[piece(j)] = (cg[piece(j)].astype(F32) + arrived[j].astype(F32)).astype(BF16)
            send.start()

        @pl.when(f == t)
        def _():
            @pl.loop(0, F - 1 - t)
            def _(i):
                j = F - 1 - i
                hop(j, c3_up(j), cgu)

        @pl.when(f == F - 1 - t)
        def _():
            @pl.loop(0, F - 1 - t)
            def _(j):
                hop(j, c3_down(j), cgd)

    reduce_step(0)
    for o in range(1, G):
        for copy in sb_cross(o, mate(o), g):
            copy.start()
    home.append(pltpu.make_async_copy(sres.at[0, g], spo.at[:, :, cols(g)], loc.at[1]))
    home.append(pltpu.make_async_copy(sres.at[4, g], cqgrad.at[:, :, cols(g)], loc.at[2]))
    home[-2].start()
    home[-1].start()

    for t in range(1, max(F - 1, G - 1)):
        if t + 1 < G:
            temporal_chunk(t + 1)
            temporal_home(t + 1)
        if t < F - 1:
            reduce_step(t)

    for i in range(G):
        at = pl.ds(pl.multiple_of((f * G + i) * RP, 8), R)
        for b in range(2):
            fin[i, b] = cacc[b, at, :]

    @pl.when(f > 0)
    def _():
        c3_up(f).wait_recv()
        fin[...] += cgu[f].astype(F32)

    @pl.when(f < F - 1)
    def _():
        c3_down(f).wait_recv()
        fin[...] += cgd[f].astype(F32)

    def c4(o, i, src_i):
        return remote(fin.at[i], capgrad.at[:, :, cols(src_i)], c4_s.at[o], c4_r.at[o], at_mate(i))

    for o in range(1, G):
        c4(o, mate(o), g).start()
    home.append(pltpu.make_async_copy(fin.at[g], capgrad.at[:, :, cols(g)], loc.at[3]))
    home[-1].start()

    for o in range(1, G):
        i = mate_from(o)
        sb_grads(o, i, i).wait_recv()
        for copy in sb_cross(o, i, i):
            copy.wait_recv()
    for copy in home:
        copy.wait()

    @pl.loop(0, G)
    def _(c):
        for o in range(1, F):
            j = line_from(o)
            for copy in tb(c, o, j, j):
                copy.wait_recv()

    shape3 = (F, pix, W)
    tok = (
        dev * T
        + lax.broadcasted_iota(jnp.int32, shape3, 0) * pix
        + lax.broadcasted_iota(jnp.int32, shape3, 1)
    )
    for c in range(G):
        at = slice(c * W, (c + 1) * W)
        total = spo[:, :, at].astype(F32) + tmo[:, :, at].astype(F32)
        mixed[:, :, at] = jnp.where(tok < live, total, 0.0).astype(BF16)

    for o in range(1, G):
        i = mate_from(o)
        c4(o, i, i).wait_recv()

    for o in range(1, G):
        c1(o).wait_send()
        for copy in s_out(o):
            copy.wait_send()
        sb_grads(o, mate(o), g).wait_send()
        for copy in sb_cross(o, mate(o), g):
            copy.wait_send()
        c4(o, mate(o), g).wait_send()

    @pl.when(f < F - 1)
    def _():
        @pl.loop(0, F)
        def _(i):
            @pl.when(i <= f)
            def _():
                up(i).wait_send()

            @pl.when(i > f)
            def _():
                c3_up(i).wait_send()

    @pl.when(f > 0)
    def _():
        @pl.loop(0, F)
        def _(i):
            @pl.when(i >= f)
            def _():
                down(i).wait_send()

            @pl.when(i < f)
            def _():
                c3_down(i).wait_send()

    @pl.loop(0, G)
    def _(c):
        for o in range(1, F):
            for copy in t_out(c, o):
                copy.wait_send()
            for copy in tb(c, o, line(o), f):
                copy.wait_send()


def local(spatial_qkv, temporal_qkv, cross_query, caption_kv, out_grad, live_tokens, caption_len):
    devices = lax.axis_size("seq")
    rows, width = out_grad.shape
    G = P_SIZE // rows
    F = devices // G
    pix = rows // F
    W = width // G
    HC = W // HDIM
    R = caption_kv.shape[0]
    RP = (R + 7) // 8 * 8
    S = G * F
    KP = S * RP
    keys = max(KP, G * rows)
    geo = (G, F, pix, W, HC, R, RP)
    dma = pltpu.SemaphoreType.DMA
    any_spec = pl.BlockSpec(memory_space=pl.ANY)
    smem = pl.BlockSpec(memory_space=pltpu.SMEM)
    vmem = pl.BlockSpec(memory_space=pltpu.VMEM)
    mixed, sgrad, tgrad, cqgrad, capgrad = pl.pallas_call(
        functools.partial(kernel, geo),
        out_shape=(
            jax.ShapeDtypeStruct((F, pix, width), BF16),
            jax.ShapeDtypeStruct((3, F, pix, width), BF16),
            jax.ShapeDtypeStruct((3, F, pix, width), BF16),
            jax.ShapeDtypeStruct((F, pix, width), BF16),
            jax.ShapeDtypeStruct((2, R, width), F32),
        ),
        in_specs=[smem, smem] + [any_spec] * 5,
        out_specs=(vmem, any_spec, any_spec, any_spec, any_spec),
        scratch_shapes=[
            pltpu.VMEM((5, G, F, pix, W), BF16),
            pltpu.VMEM((5, G, F, pix, W), BF16),
            pltpu.VMEM((G, 4, F, pix, W), BF16),
            pltpu.VMEM((G, 4, F, pix, W), BF16),
            pltpu.VMEM((S, 2, R, W), BF16),
            pltpu.VMEM((2, KP, W), F32),
            pltpu.VMEM((2, KP, W), BF16),
            pltpu.VMEM((KP, HDIM), F32),
            pltpu.VMEM((2, KP, W), F32),
            pltpu.VMEM((S, 2, R, W), BF16),
            pltpu.VMEM((F, G, 2, R, W), BF16),
            pltpu.VMEM((F, G, 2, R, W), BF16),
            pltpu.VMEM((G, 2, R, W), F32),
            pltpu.VMEM((F, pix, width), BF16),
            pltpu.VMEM((F, pix, width), BF16),
            pltpu.VMEM((keys, G * rows), BF16),
            pltpu.VMEM((keys, G * rows), BF16),
            pltpu.VMEM((rows, rows), F32),
            dma((4 + 2 * G,)),
            dma((G, F, 2)), dma((G, F, 2)),
            dma((G, F, 2)), dma((G, F, 2)),
            dma((G, 3)), dma((G, 3)),
            dma((G, 3)), dma((G, 3)),
            dma((G,)), dma((G,)),
            dma((2, F)), dma((2, F)),
            dma((2, F)), dma((2, F)),
            dma((G,)), dma((G,)),
        ],
        compiler_params=pltpu.CompilerParams(
            collective_id=0, has_side_effects=True, vmem_limit_bytes=60 * 1024 * 1024
        ),
    )(
        live_tokens,
        caption_len,
        spatial_qkv.reshape(3, F, pix, width),
        temporal_qkv.reshape(3, F, pix, width),
        cross_query.reshape(F, pix, width),
        jnp.swapaxes(caption_kv, 0, 1),
        out_grad.reshape(F, pix, width),
    )
    return (
        mixed.reshape(rows, width),
        sgrad.reshape(3, rows, width),
        tgrad.reshape(3, rows, width),
        cqgrad.reshape(rows, width),
        jnp.swapaxes(capgrad, 0, 1),
    )


def solution(mesh):
    placed = (
        P(None, ("dp", "seq"), None),
        P(None, ("dp", "seq"), None),
        P(("dp", "seq"), None),
        P(("dp", "seq"), None, None),
        P(("dp", "seq"), None),
        P("dp"),
        P("dp"),
    )
    return jax.shard_map(
        local,
        mesh=mesh,
        in_specs=placed,
        out_specs=(
            P(("dp", "seq"), None),
            P(None, ("dp", "seq"), None),
            P(None, ("dp", "seq"), None),
            P(("dp", "seq"), None),
            P(("dp", "seq"), None, None),
        ),
        check_vma=False,
    )
```

```python
import functools

import jax
import jax.numpy as jnp
from jax import lax
from jax.experimental import pallas as pl
from jax.experimental.pallas import tpu as pltpu
from jax.sharding import PartitionSpec as P

HDIM = 128
P_SIZE = 512
F32 = jnp.float32
BF16 = jnp.bfloat16
LOW = -1e30


def dot_nt(a, b):
    return lax.dot_general(a, b, (((1,), (1,)), ((), ())), preferred_element_type=F32)


def dot_tn(a, b):
    return lax.dot_general(a, b, (((0,), (0,)), ((), ())), preferred_element_type=F32)


def dot_nn(a, b):
    return lax.dot_general(a, b, (((1,), (0,)), ((), ())), preferred_element_type=F32)


def flat(x):
    rows = 1
    for n in x.shape[:-1]:
        rows *= n
    if x.shape[-2] % 16:
        return x.astype(F32).reshape(rows, x.shape[-1]).astype(BF16)
    return x.reshape(rows, x.shape[-1])


def unflat(x, shape):
    if shape[-2] % 16:
        return x.reshape(shape).astype(BF16)
    return x.astype(BF16).reshape(shape)


def slopes(q, k, v, g, scale, bias):
    s = dot_nt(k, q) * scale
    if bias is not None:
        s = s + bias
    p = jnp.exp(s - jnp.max(s, axis=0, keepdims=True))
    w = p * (1.0 / jnp.sum(p, axis=0, keepdims=True))
    dp = dot_nt(v, g)
    delta = jnp.sum(w * dp, axis=0, keepdims=True)
    return w.astype(BF16), (w * (dp - delta)).astype(BF16)


def kernel(
    geo,
    live_ref, clen_ref, sqkv, tqkv, cq, cap_in, og,
    mixed, sgrad, tgrad, cqgrad, capgrad,
    srecv, sres, trecv, tres, crecv, cf, ckv, cbias, cacc, cg, cgu, cgd, fin, spo, tmo, wbuf, dbuf, tbias, cap,
    loc, t_s, t_r, tb_s, tb_r, s_s, s_r, sb_s, sb_r, c1_s, c1_r, c2_s, c2_r, c3_s, c3_r, c4_s, c4_r,
):
    G, F, pix, W, HC, R, RP = geo
    S = G * F
    KP = S * RP
    T = F * pix
    scale = HDIM ** (-0.5)
    dev = lax.axis_index("seq")
    f = dev // G
    g = dev % G
    live = live_ref[0]
    clen = clen_ref[0]

    def cols(i):
        return pl.ds(pl.multiple_of(i * W, 128), W)

    def hcols(h):
        return pl.ds(pl.multiple_of(h * HDIM, 128), HDIM)

    def mate(o):
        return (g + o) % G

    def mate_from(o):
        return (g + G - o) % G

    def line(o):
        return (f + o) % F

    def line_from(o):
        return (f + F - o) % F

    def at_mate(i):
        return f * G + i

    def at_line(i):
        return i * G + g

    def remote(src, dst, ss, rs, to):
        return pltpu.make_async_remote_copy(
            src_ref=src, dst_ref=dst, send_sem=ss, recv_sem=rs,
            device_id={"seq": to}, device_id_type=pl.DeviceIdType.MESH,
        )

    barrier = pltpu.get_barrier_semaphore()
    for o in range(1, G):
        pl.semaphore_signal(barrier, inc=1, device_id={"seq": at_mate(mate(o))}, device_id_type=pl.DeviceIdType.MESH)
    for o in range(1, F):
        pl.semaphore_signal(barrier, inc=1, device_id={"seq": at_line(line(o))}, device_id_type=pl.DeviceIdType.MESH)

    for i in range(2):
        cap[i] = cap_in[:, i, :]

    local = [
        pltpu.make_async_copy(cap.at[:, :, cols(g)], crecv.at[dev], loc.at[0]),
        pltpu.make_async_copy(sqkv.at[:, :, :, cols(g)], srecv.at[pl.ds(0, 3), g], loc.at[1]),
        pltpu.make_async_copy(og.at[:, :, cols(g)], srecv.at[3, g], loc.at[2]),
        pltpu.make_async_copy(cq.at[:, :, cols(g)], srecv.at[4, g], loc.at[3]),
    ]
    for c in range(G):
        local.append(pltpu.make_async_copy(tqkv.at[:, f, :, cols(c)], trecv.at[c, pl.ds(0, 3), f], loc.at[4 + 2 * c]))
        local.append(pltpu.make_async_copy(og.at[f, :, cols(c)], trecv.at[c, 3, f], loc.at[5 + 2 * c]))
    for copy in local:
        copy.start()
    pl.semaphore_wait(barrier, G + F - 2)

    def c1(o):
        return remote(cap.at[:, :, cols(mate(o))], crecv.at[dev], c1_s.at[o], c1_r.at[o], at_mate(mate(o)))

    def c1_in(o):
        i = mate_from(o)
        return remote(cap.at[:, :, cols(i)], crecv.at[at_mate(i)], c1_s.at[o], c1_r.at[o], at_mate(i))

    def t_out(c, o):
        j = line(o)
        return (
            remote(tqkv.at[:, j, :, cols(c)], trecv.at[c, pl.ds(0, 3), f], t_s.at[c, o, 0], t_r.at[c, o, 0], at_line(j)),
            remote(og.at[j, :, cols(c)], trecv.at[c, 3, f], t_s.at[c, o, 1], t_r.at[c, o, 1], at_line(j)),
        )

    def t_in(c, o):
        j = line_from(o)
        return (
            remote(tqkv.at[:, j, :, cols(c)], trecv.at[c, pl.ds(0, 3), j], t_s.at[c, o, 0], t_r.at[c, o, 0], at_line(j)),
            remote(og.at[j, :, cols(c)], trecv.at[c, 3, j], t_s.at[c, o, 1], t_r.at[c, o, 1], at_line(j)),
        )

    def s_out(o):
        i = mate(o)
        return (
            remote(sqkv.at[:, :, :, cols(i)], srecv.at[pl.ds(0, 3), g], s_s.at[o, 0], s_r.at[o, 0], at_mate(i)),
            remote(og.at[:, :, cols(i)], srecv.at[3, g], s_s.at[o, 1], s_r.at[o, 1], at_mate(i)),
            remote(cq.at[:, :, cols(i)], srecv.at[4, g], s_s.at[o, 2], s_r.at[o, 2], at_mate(i)),
        )

    def s_in(o):
        i = mate_from(o)
        return (
            remote(sqkv.at[:, :, :, cols(i)], srecv.at[pl.ds(0, 3), i], s_s.at[o, 0], s_r.at[o, 0], at_mate(i)),
            remote(og.at[:, :, cols(i)], srecv.at[3, i], s_s.at[o, 1], s_r.at[o, 1], at_mate(i)),
            remote(cq.at[:, :, cols(i)], srecv.at[4, i], s_s.at[o, 2], s_r.at[o, 2], at_mate(i)),
        )

    def send_chunk(c):
        for o in range(1, F):
            for copy in t_out(c, o):
                copy.start()

    for o in range(1, G):
        c1(o).start()
    for o in range(1, max(F, G)):
        if o < F:
            for copy in t_out(0, o):
                copy.start()
        if o < G:
            for copy in s_out(o):
                copy.start()

    def piece(i):
        return pl.ds(i * G, G)

    def up(i):
        return remote(crecv.at[piece(i)], crecv.at[piece(i)], c2_s.at[0, i], c2_r.at[0, i], at_line(line(1)))

    def down(i):
        return remote(crecv.at[piece(i)], crecv.at[piece(i)], c2_s.at[1, i], c2_r.at[1, i], at_line(line_from(1)))

    def gather_step(t):
        @pl.when(f >= t)
        def _():
            if t > 0:
                up(f - t).wait_recv()

            @pl.when(f < F - 1)
            def _():
                up(f - t).start()

        @pl.when(f + t < F)
        def _():
            if t > 0:
                down(f + t).wait_recv()

            @pl.when(f > 0)
            def _():
                down(f + t).start()

    local[0].wait()
    for o in range(1, G):
        c1_in(o).wait_recv()
    gather_step(0)
    send_chunk(1)

    cf[...] = jnp.zeros(cf.shape, F32)
    cbias[...] = jnp.full(cbias.shape, LOW, F32)

    def live_rows(x, first):
        ids = first + lax.broadcasted_iota(jnp.int32, x.shape, 0)
        return jnp.where(ids < live, x.astype(F32), 0.0).astype(BF16)

    def many(k, v, q, gr, keys, bias):
        for b in range(G):
            rows = slice(b * T, (b + 1) * T)
            w, d = slopes(q[rows], k, v, gr[rows], scale, bias)
            wbuf[pl.ds(0, keys), rows] = w
            dbuf[pl.ds(0, keys), rows] = d
        w = wbuf[pl.ds(0, keys), :]
        d = dbuf[pl.ds(0, keys), :]
        return dot_tn(w, v), dot_tn(d, k) * scale, dot_nn(d, q) * scale, dot_nn(w, gr)

    rk = lax.broadcasted_iota(jnp.int32, (T, T), 0)
    rq = lax.broadcasted_iota(jnp.int32, (T, T), 1)
    shift = pix.bit_length() - 1
    first = g * T + f * pix
    key_token = (rk >> shift) * P_SIZE + (rk & (pix - 1)) + first
    same = ((rk & (pix - 1)) == (rq & (pix - 1))) & (key_token < live)
    tbias[...] = jnp.where(same, 0.0, LOW)

    def tb(c, o, j, src_j):
        return (
            remote(tres.at[c, 0, j], tmo.at[src_j, :, cols(c)], tb_s.at[c, o, 0], tb_r.at[c, o, 0], at_line(j)),
            remote(tres.at[c, pl.ds(1, 3), j], tgrad.at[:, src_j, :, cols(c)], tb_s.at[c, o, 1], tb_r.at[c, o, 1], at_line(j)),
        )

    tblock = (F, pix, HDIM)
    home = []

    def temporal_chunk(c):
        for o in range(1, F):
            for copy in t_in(c, o):
                copy.wait_recv()
        rd = lax.broadcasted_iota(jnp.int32, (T, HDIM), 0)
        t_live = ((rd >> shift) * P_SIZE + (rd & (pix - 1)) + first) < live
        for h in range(HC):
            at = pl.ds(h * HDIM, HDIM)
            q, k, v, gr = (flat(trecv[c, i, :, :, at]) for i in range(4))
            gr = jnp.where(t_live, gr.astype(F32), 0.0).astype(BF16)
            w, d = slopes(q, k, v, gr, scale, tbias[...])
            tres[c, 0, :, :, at] = unflat(dot_tn(w, v), tblock)
            tres[c, 1, :, :, at] = unflat(dot_tn(d, k) * scale, tblock)
            tres[c, 2, :, :, at] = unflat(dot_nn(d, q) * scale, tblock)
            tres[c, 3, :, :, at] = unflat(dot_nn(w, gr), tblock)
        for o in range(1, F):
            for copy in tb(c, o, line(o), f):
                copy.start()

    def temporal_home(c):
        mine = [
            pltpu.make_async_copy(tres.at[c, 0, f], tmo.at[f, :, cols(c)], loc.at[4 + 2 * c]),
            pltpu.make_async_copy(tres.at[c, pl.ds(1, 3), f], tgrad.at[:, f, :, cols(c)], loc.at[5 + 2 * c]),
        ]
        for copy in mine:
            copy.start()
        home.extend(mine)

    for c in range(G):
        local[4 + 2 * c].wait()
        local[5 + 2 * c].wait()
    for t in range(1, max(F - 1, 3)):
        if t <= 2:
            temporal_chunk(t - 1)
            temporal_home(t - 1)
        if t < F - 1:
            gather_step(t)
        if t + 1 < G:
            send_chunk(t + 1)
    for c in range(max(F - 1, 3) + 1, G):
        send_chunk(c)

    for copy in local[1:4]:
        copy.wait()
    for o in range(1, G):
        for copy in s_in(o):
            copy.wait_recv()

    block = (G, F, pix, HDIM)

    @pl.loop(0, HC)
    def _(h):
        at = hcols(h)
        q, k, v = (flat(srecv[i, :, :, :, at]) for i in range(3))
        gr = live_rows(flat(srecv[3, :, :, :, at]), f * (G * T))
        out, dq, dk, dv = many(k, v, q, gr, G * T, None)
        sres[0, :, :, :, at] = unflat(out, block)
        sres[1, :, :, :, at] = unflat(dq, block)
        sres[2, :, :, :, at] = unflat(dk, block)
        sres[3, :, :, :, at] = unflat(dv, block)

    def sb_grads(o, i, src_i):
        return remote(sres.at[pl.ds(1, 3), i], sgrad.at[:, :, :, cols(src_i)], sb_s.at[o, 0], sb_r.at[o, 0], at_mate(i))

    def sb_cross(o, i, src_i):
        return (
            remote(sres.at[0, i], spo.at[:, :, cols(src_i)], sb_s.at[o, 1], sb_r.at[o, 1], at_mate(i)),
            remote(sres.at[4, i], cqgrad.at[:, :, cols(src_i)], sb_s.at[o, 2], sb_r.at[o, 2], at_mate(i)),
        )

    for o in range(1, G):
        sb_grads(o, mate(o), g).start()
    home.append(pltpu.make_async_copy(sres.at[pl.ds(1, 3), g], sgrad.at[:, :, :, cols(g)], loc.at[0]))
    home[-1].start()

    temporal_chunk(2)
    temporal_home(2)

    @pl.when(f == F - 1)
    def _():
        up(0).wait_recv()

    @pl.when(f == 0)
    def _():
        down(F - 1).wait_recv()

    @pl.loop(0, S)
    def _(s):
        at = pl.ds(pl.multiple_of(s * RP, 8), R)
        for i in range(2):
            cf[i, at, :] = crecv[s, i].astype(F32)
        ids = s * R + lax.broadcasted_iota(jnp.int32, (R, HDIM), 0)
        cbias[at, :] = jnp.where(ids < clen, 0.0, LOW)

    ckv[...] = cf[...].astype(BF16)

    @pl.loop(0, HC)
    def _(h):
        at = hcols(h)
        q = flat(srecv[4, :, :, :, at])
        gr = live_rows(flat(srecv[3, :, :, :, at]), f * (G * T))
        k = ckv[0, :, at]
        v = ckv[1, :, at]
        out, dq, dk, dv = many(k, v, q, gr, KP, cbias[...])
        total = flat(sres[0, :, :, :, at]).astype(F32) + out
        sres[0, :, :, :, at] = unflat(total, block)
        sres[4, :, :, :, at] = unflat(dq, block)
        cacc[0, :, at] = dk
        cacc[1, :, at] = dv

    @pl.loop(0, S)
    def _(s):
        at = pl.ds(pl.multiple_of(s * RP, 8), R)
        for i in range(2):
            cg[s, i] = cacc[i, at, :].astype(BF16)

    def c3_up(j):
        return remote(cg.at[piece(j)], cgu.at[j], c3_s.at[0, j], c3_r.at[0, j], at_line(line(1)))

    def c3_down(j):
        return remote(cg.at[piece(j)], cgd.at[j], c3_s.at[1, j], c3_r.at[1, j], at_line(line_from(1)))

    def reduce_step(t):
        def hop(j, send, arrived):
            if t > 0:
                send.wait_recv()
                cg[piece(j)] = (cg[piece(j)].astype(F32) + arrived[j].astype(F32)).astype(BF16)
            send.start()

        @pl.when(f == t)
        def _():
            @pl.loop(0, F - 1 - t)
            def _(i):
                j = F - 1 - i
                hop(j, c3_up(j), cgu)

        @pl.when(f == F - 1 - t)
        def _():
            @pl.loop(0, F - 1 - t)
            def _(j):
                hop(j, c3_down(j), cgd)

    reduce_step(0)
    for o in range(1, G):
        for copy in sb_cross(o, mate(o), g):
            copy.start()
    home.append(pltpu.make_async_copy(sres.at[0, g], spo.at[:, :, cols(g)], loc.at[1]))
    home.append(pltpu.make_async_copy(sres.at[4, g], cqgrad.at[:, :, cols(g)], loc.at[2]))
    home[-2].start()
    home[-1].start()

    for t in range(1, max(F - 1, G - 2)):
        if t + 2 < G:
            temporal_chunk(t + 2)
            temporal_home(t + 2)
        if t < F - 1:
            reduce_step(t)

    for i in range(G):
        at = pl.ds(pl.multiple_of((f * G + i) * RP, 8), R)
        for b in range(2):
            fin[i, b] = cacc[b, at, :]

    @pl.when(f > 0)
    def _():
        c3_up(f).wait_recv()
        fin[...] += cgu[f].astype(F32)

    @pl.when(f < F - 1)
    def _():
        c3_down(f).wait_recv()
        fin[...] += cgd[f].astype(F32)

    def c4(o, i, src_i):
        return remote(fin.at[i], capgrad.at[:, :, cols(src_i)], c4_s.at[o], c4_r.at[o], at_mate(i))

    for o in range(1, G):
        c4(o, mate(o), g).start()
    home.append(pltpu.make_async_copy(fin.at[g], capgrad.at[:, :, cols(g)], loc.at[3]))
    home[-1].start()

    for o in range(1, G):
        i = mate_from(o)
        sb_grads(o, i, i).wait_recv()
        for copy in sb_cross(o, i, i):
            copy.wait_recv()
    for copy in home:
        copy.wait()

    @pl.loop(0, G)
    def _(c):
        for o in range(1, F):
            j = line_from(o)
            for copy in tb(c, o, j, j):
                copy.wait_recv()

    shape3 = (F, pix, W)
    tok = (
        dev * T
        + lax.broadcasted_iota(jnp.int32, shape3, 0) * pix
        + lax.broadcasted_iota(jnp.int32, shape3, 1)
    )
    for c in range(G):
        at = slice(c * W, (c + 1) * W)
        total = spo[:, :, at].astype(F32) + tmo[:, :, at].astype(F32)
        mixed[:, :, at] = jnp.where(tok < live, total, 0.0).astype(BF16)

    for o in range(1, G):
        i = mate_from(o)
        c4(o, i, i).wait_recv()

    for o in range(1, G):
        c1(o).wait_send()
        for copy in s_out(o):
            copy.wait_send()
        sb_grads(o, mate(o), g).wait_send()
        for copy in sb_cross(o, mate(o), g):
            copy.wait_send()
        c4(o, mate(o), g).wait_send()

    @pl.when(f < F - 1)
    def _():
        @pl.loop(0, F)
        def _(i):
            @pl.when(i <= f)
            def _():
                up(i).wait_send()

            @pl.when(i > f)
            def _():
                c3_up(i).wait_send()

    @pl.when(f > 0)
    def _():
        @pl.loop(0, F)
        def _(i):
            @pl.when(i >= f)
            def _():
                down(i).wait_send()

            @pl.when(i < f)
            def _():
                c3_down(i).wait_send()

    @pl.loop(0, G)
    def _(c):
        for o in range(1, F):
            for copy in t_out(c, o):
                copy.wait_send()
            for copy in tb(c, o, line(o), f):
                copy.wait_send()


def hand_on(*refs):
    n = (len(refs) - 2) // 2
    srcs, caps, dsts, capo, sem = refs[:n], refs[n], refs[n + 1 : 2 * n + 1], refs[2 * n + 1], refs[-1]
    copies = []
    for src, dst in zip(srcs, dsts):
        if src.ndim == 3:
            copies += [(src.at[i], dst.at[i]) for i in range(src.shape[0])]
        else:
            half = src.shape[0] // 2
            copies += [(src.at[pl.ds(i * half, half)], dst.at[pl.ds(i * half, half)]) for i in range(2)]
    copies = [pltpu.make_async_copy(a, b, sem.at[i]) for i, (a, b) in enumerate(copies)]
    for copy in copies:
        copy.start()
    for i in range(2):
        capo[:, i, :] = caps[i]
    for copy in copies:
        copy.wait()


def local(spatial_qkv, temporal_qkv, cross_query, caption_kv, out_grad, live_tokens, caption_len):
    devices = lax.axis_size("seq")
    rows, width = out_grad.shape
    G = P_SIZE // rows
    F = devices // G
    pix = rows // F
    W = width // G
    HC = W // HDIM
    R = caption_kv.shape[0]
    RP = (R + 7) // 8 * 8
    S = G * F
    KP = S * RP
    keys = max(KP, G * rows)
    geo = (G, F, pix, W, HC, R, RP)
    dma = pltpu.SemaphoreType.DMA
    any_spec = pl.BlockSpec(memory_space=pl.ANY)
    smem = pl.BlockSpec(memory_space=pltpu.SMEM)
    vmem = pl.BlockSpec(memory_space=pltpu.VMEM)
    mixed, sgrad, tgrad, cqgrad, capgrad = pl.pallas_call(
        functools.partial(kernel, geo),
        out_shape=(
            jax.ShapeDtypeStruct((F, pix, width), BF16),
            jax.ShapeDtypeStruct((3, F, pix, width), BF16),
            jax.ShapeDtypeStruct((3, F, pix, width), BF16),
            jax.ShapeDtypeStruct((F, pix, width), BF16),
            jax.ShapeDtypeStruct((2, R, width), F32),
        ),
        in_specs=[smem, smem, any_spec, any_spec, any_spec, vmem, any_spec],
        out_specs=(vmem, any_spec, any_spec, any_spec, any_spec),
        scratch_shapes=[
            pltpu.VMEM((5, G, F, pix, W), BF16),
            pltpu.VMEM((5, G, F, pix, W), BF16),
            pltpu.VMEM((G, 4, F, pix, W), BF16),
            pltpu.VMEM((G, 4, F, pix, W), BF16),
            pltpu.VMEM((S, 2, R, W), BF16),
            pltpu.VMEM((2, KP, W), F32),
            pltpu.VMEM((2, KP, W), BF16),
            pltpu.VMEM((KP, HDIM), F32),
            pltpu.VMEM((2, KP, W), F32),
            pltpu.VMEM((S, 2, R, W), BF16),
            pltpu.VMEM((F, G, 2, R, W), BF16),
            pltpu.VMEM((F, G, 2, R, W), BF16),
            pltpu.VMEM((G, 2, R, W), F32),
            pltpu.VMEM((F, pix, width), BF16),
            pltpu.VMEM((F, pix, width), BF16),
            pltpu.VMEM((keys, G * rows), BF16),
            pltpu.VMEM((keys, G * rows), BF16),
            pltpu.VMEM((rows, rows), F32),
            pltpu.VMEM((2, R, width), BF16),
            dma((4 + 2 * G,)),
            dma((G, F, 2)), dma((G, F, 2)),
            dma((G, F, 2)), dma((G, F, 2)),
            dma((G, 3)), dma((G, 3)),
            dma((G, 3)), dma((G, 3)),
            dma((G,)), dma((G,)),
            dma((2, F)), dma((2, F)),
            dma((2, F)), dma((2, F)),
            dma((G,)), dma((G,)),
        ],
        compiler_params=pltpu.CompilerParams(
            collective_id=0, has_side_effects=True, vmem_limit_bytes=60 * 1024 * 1024
        ),
    )(
        live_tokens,
        caption_len,
        spatial_qkv.reshape(3, F, pix, width),
        temporal_qkv.reshape(3, F, pix, width),
        cross_query.reshape(F, pix, width),
        caption_kv,
        out_grad.reshape(F, pix, width),
    )
    return pl.pallas_call(
        hand_on,
        out_shape=(
            jax.ShapeDtypeStruct((rows, width), BF16),
            jax.ShapeDtypeStruct((3, rows, width), BF16),
            jax.ShapeDtypeStruct((3, rows, width), BF16),
            jax.ShapeDtypeStruct((rows, width), BF16),
            jax.ShapeDtypeStruct((R, 2, width), F32),
        ),
        in_specs=[any_spec] * 4 + [vmem],
        out_specs=(any_spec, any_spec, any_spec, any_spec, vmem),
        scratch_shapes=[dma((10,))],
        compiler_params=pltpu.CompilerParams(vmem_limit_bytes=60 * 1024 * 1024),
    )(
        mixed.reshape(rows, width),
        sgrad.reshape(3, rows, width),
        tgrad.reshape(3, rows, width),
        cqgrad.reshape(rows, width),
        capgrad,
    )


def solution(mesh):
    placed = (
        P(None, ("dp", "seq"), None),
        P(None, ("dp", "seq"), None),
        P(("dp", "seq"), None),
        P(("dp", "seq"), None, None),
        P(("dp", "seq"), None),
        P("dp"),
        P("dp"),
    )
    return jax.shard_map(
        local,
        mesh=mesh,
        in_specs=placed,
        out_specs=(
            P(("dp", "seq"), None),
            P(None, ("dp", "seq"), None),
            P(None, ("dp", "seq"), None),
            P(("dp", "seq"), None),
            P(("dp", "seq"), None, None),
        ),
        check_vma=False,
    )
```

```python
import functools

import jax
import jax.numpy as jnp
from jax import lax
from jax.experimental import pallas as pl
from jax.experimental.pallas import tpu as pltpu
from jax.sharding import PartitionSpec as P

HDIM = 128
P_SIZE = 512
F32 = jnp.float32
BF16 = jnp.bfloat16
LOW = -1e30


def dot_nt(a, b):
    return lax.dot_general(a, b, (((1,), (1,)), ((), ())), preferred_element_type=F32)


def dot_tn(a, b):
    return lax.dot_general(a, b, (((0,), (0,)), ((), ())), preferred_element_type=F32)


def dot_nn(a, b):
    return lax.dot_general(a, b, (((1,), (0,)), ((), ())), preferred_element_type=F32)


def flat(x):
    rows = 1
    for n in x.shape[:-1]:
        rows *= n
    if x.shape[-2] % 16:
        return x.astype(F32).reshape(rows, x.shape[-1]).astype(BF16)
    return x.reshape(rows, x.shape[-1])


def unflat(x, shape):
    if shape[-2] % 16:
        return x.reshape(shape).astype(BF16)
    return x.astype(BF16).reshape(shape)


def slopes(q, k, v, g, scale, bias):
    s = dot_nt(k, q) * scale
    if bias is not None:
        s = s + bias
    p = jnp.exp(s - jnp.max(s, axis=0, keepdims=True))
    w = p * (1.0 / jnp.sum(p, axis=0, keepdims=True))
    dp = dot_nt(v, g)
    delta = jnp.sum(w * dp, axis=0, keepdims=True)
    return w.astype(BF16), (w * (dp - delta)).astype(BF16)


def kernel(
    geo,
    live_ref, clen_ref, sqkv, tqkv, cq, cap_in, og,
    mixed, sgrad, tgrad, cqgrad, capgrad,
    srecv, sres, trecv, tres, crecv, cf, ckv, cbias, cacc, cg, cgu, cgd, fin, spo, tmo, wbuf, dbuf, tbias, cap,
    loc, t_s, t_r, tb_s, tb_r, s_s, s_r, sb_s, sb_r, c1_s, c1_r, c2_s, c2_r, c3_s, c3_r, c4_s, c4_r,
):
    G, F, pix, W, HC, R, RP = geo
    S = G * F
    KP = S * RP
    T = F * pix
    scale = HDIM ** (-0.5)
    dev = lax.axis_index("seq")
    f = dev // G
    g = dev % G
    live = live_ref[0]
    clen = clen_ref[0]

    def cols(i):
        return pl.ds(pl.multiple_of(i * W, 128), W)

    def hcols(h):
        return pl.ds(pl.multiple_of(h * HDIM, 128), HDIM)

    def mate(o):
        return (g + o) % G

    def mate_from(o):
        return (g + G - o) % G

    def line(o):
        return (f + o) % F

    def line_from(o):
        return (f + F - o) % F

    def at_mate(i):
        return f * G + i

    def at_line(i):
        return i * G + g

    def remote(src, dst, ss, rs, to):
        return pltpu.make_async_remote_copy(
            src_ref=src, dst_ref=dst, send_sem=ss, recv_sem=rs,
            device_id={"seq": to}, device_id_type=pl.DeviceIdType.MESH,
        )

    barrier = pltpu.get_barrier_semaphore()
    for o in range(1, G):
        pl.semaphore_signal(barrier, inc=1, device_id={"seq": at_mate(mate(o))}, device_id_type=pl.DeviceIdType.MESH)
    for o in range(1, F):
        pl.semaphore_signal(barrier, inc=1, device_id={"seq": at_line(line(o))}, device_id_type=pl.DeviceIdType.MESH)

    for i in range(2):
        cap[i] = cap_in[:, i, :]

    local = [
        pltpu.make_async_copy(cap.at[:, :, cols(g)], crecv.at[dev], loc.at[0]),
        pltpu.make_async_copy(sqkv.at[:, :, :, cols(g)], srecv.at[pl.ds(0, 3), g], loc.at[1]),
        pltpu.make_async_copy(og.at[:, :, cols(g)], srecv.at[3, g], loc.at[2]),
        pltpu.make_async_copy(cq.at[:, :, cols(g)], srecv.at[4, g], loc.at[3]),
    ]
    for c in range(G):
        local.append(pltpu.make_async_copy(tqkv.at[:, f, :, cols(c)], trecv.at[c, pl.ds(0, 3), f], loc.at[4 + 2 * c]))
        local.append(pltpu.make_async_copy(og.at[f, :, cols(c)], trecv.at[c, 3, f], loc.at[5 + 2 * c]))
    for copy in local:
        copy.start()
    pl.semaphore_wait(barrier, G + F - 2)

    def c1(o):
        return remote(cap.at[:, :, cols(mate(o))], crecv.at[dev], c1_s.at[o], c1_r.at[o], at_mate(mate(o)))

    def c1_in(o):
        i = mate_from(o)
        return remote(cap.at[:, :, cols(i)], crecv.at[at_mate(i)], c1_s.at[o], c1_r.at[o], at_mate(i))

    def t_out(c, o):
        j = line(o)
        return (
            remote(tqkv.at[:, j, :, cols(c)], trecv.at[c, pl.ds(0, 3), f], t_s.at[c, o, 0], t_r.at[c, o, 0], at_line(j)),
            remote(og.at[j, :, cols(c)], trecv.at[c, 3, f], t_s.at[c, o, 1], t_r.at[c, o, 1], at_line(j)),
        )

    def t_in(c, o):
        j = line_from(o)
        return (
            remote(tqkv.at[:, j, :, cols(c)], trecv.at[c, pl.ds(0, 3), j], t_s.at[c, o, 0], t_r.at[c, o, 0], at_line(j)),
            remote(og.at[j, :, cols(c)], trecv.at[c, 3, j], t_s.at[c, o, 1], t_r.at[c, o, 1], at_line(j)),
        )

    def s_out(o):
        i = mate(o)
        return (
            remote(sqkv.at[:, :, :, cols(i)], srecv.at[pl.ds(0, 3), g], s_s.at[o, 0], s_r.at[o, 0], at_mate(i)),
            remote(og.at[:, :, cols(i)], srecv.at[3, g], s_s.at[o, 1], s_r.at[o, 1], at_mate(i)),
            remote(cq.at[:, :, cols(i)], srecv.at[4, g], s_s.at[o, 2], s_r.at[o, 2], at_mate(i)),
        )

    def s_in(o):
        i = mate_from(o)
        return (
            remote(sqkv.at[:, :, :, cols(i)], srecv.at[pl.ds(0, 3), i], s_s.at[o, 0], s_r.at[o, 0], at_mate(i)),
            remote(og.at[:, :, cols(i)], srecv.at[3, i], s_s.at[o, 1], s_r.at[o, 1], at_mate(i)),
            remote(cq.at[:, :, cols(i)], srecv.at[4, i], s_s.at[o, 2], s_r.at[o, 2], at_mate(i)),
        )

    def send_chunk(c):
        for o in range(1, F):
            for copy in t_out(c, o):
                copy.start()

    for o in range(1, G):
        c1(o).start()
    send_chunk(0)
    for o in range(1, G):
        for copy in s_out(o):
            copy.start()

    def piece(i):
        return pl.ds(i * G, G)

    def up(i):
        return remote(crecv.at[piece(i)], crecv.at[piece(i)], c2_s.at[0, i], c2_r.at[0, i], at_line(line(1)))

    def down(i):
        return remote(crecv.at[piece(i)], crecv.at[piece(i)], c2_s.at[1, i], c2_r.at[1, i], at_line(line_from(1)))

    def gather_step(t):
        @pl.when(f >= t)
        def _():
            if t > 0:
                up(f - t).wait_recv()

            @pl.when(f < F - 1)
            def _():
                up(f - t).start()

        @pl.when(f + t < F)
        def _():
            if t > 0:
                down(f + t).wait_recv()

            @pl.when(f > 0)
            def _():
                down(f + t).start()

    local[0].wait()
    for o in range(1, G):
        c1_in(o).wait_recv()
    gather_step(0)
    send_chunk(1)

    cf[...] = jnp.zeros(cf.shape, F32)
    cbias[...] = jnp.full(cbias.shape, LOW, F32)

    def live_rows(x, first):
        ids = first + lax.broadcasted_iota(jnp.int32, x.shape, 0)
        return jnp.where(ids < live, x.astype(F32), 0.0).astype(BF16)

    def many(k, v, q, gr, keys, bias):
        for b in range(G):
            rows = slice(b * T, (b + 1) * T)
            w, d = slopes(q[rows], k, v, gr[rows], scale, bias)
            wbuf[pl.ds(0, keys), rows] = w
            dbuf[pl.ds(0, keys), rows] = d
        w = wbuf[pl.ds(0, keys), :]
        d = dbuf[pl.ds(0, keys), :]
        return dot_tn(w, v), dot_tn(d, k) * scale, dot_nn(d, q) * scale, dot_nn(w, gr)

    rk = lax.broadcasted_iota(jnp.int32, (T, T), 0)
    rq = lax.broadcasted_iota(jnp.int32, (T, T), 1)
    shift = pix.bit_length() - 1
    first = g * T + f * pix
    key_token = (rk >> shift) * P_SIZE + (rk & (pix - 1)) + first
    same = ((rk & (pix - 1)) == (rq & (pix - 1))) & (key_token < live)
    tbias[...] = jnp.where(same, 0.0, LOW)

    def tb(c, o, j, src_j):
        return (
            remote(tres.at[c, 0, j], tmo.at[src_j, :, cols(c)], tb_s.at[c, o, 0], tb_r.at[c, o, 0], at_line(j)),
            remote(tres.at[c, pl.ds(1, 3), j], tgrad.at[:, src_j, :, cols(c)], tb_s.at[c, o, 1], tb_r.at[c, o, 1], at_line(j)),
        )

    tblock = (F, pix, HDIM)
    home = []

    def temporal_chunk(c):
        for o in range(1, F):
            for copy in t_in(c, o):
                copy.wait_recv()
        rd = lax.broadcasted_iota(jnp.int32, (T, HDIM), 0)
        t_live = ((rd >> shift) * P_SIZE + (rd & (pix - 1)) + first) < live
        for h in range(HC):
            at = pl.ds(h * HDIM, HDIM)
            q, k, v, gr = (flat(trecv[c, i, :, :, at]) for i in range(4))
            gr = jnp.where(t_live, gr.astype(F32), 0.0).astype(BF16)
            w, d = slopes(q, k, v, gr, scale, tbias[...])
            tres[c, 0, :, :, at] = unflat(dot_tn(w, v), tblock)
            tres[c, 1, :, :, at] = unflat(dot_tn(d, k) * scale, tblock)
            tres[c, 2, :, :, at] = unflat(dot_nn(d, q) * scale, tblock)
            tres[c, 3, :, :, at] = unflat(dot_nn(w, gr), tblock)
        for o in range(1, F):
            for copy in tb(c, o, line(o), f):
                copy.start()

    def temporal_home(c):
        mine = [
            pltpu.make_async_copy(tres.at[c, 0, f], tmo.at[f, :, cols(c)], loc.at[4 + 2 * c]),
            pltpu.make_async_copy(tres.at[c, pl.ds(1, 3), f], tgrad.at[:, f, :, cols(c)], loc.at[5 + 2 * c]),
        ]
        for copy in mine:
            copy.start()
        home.extend(mine)

    for c in range(G):
        local[4 + 2 * c].wait()
        local[5 + 2 * c].wait()
    for t in range(1, max(F - 1, 3)):
        if t <= 2:
            temporal_chunk(t - 1)
            temporal_home(t - 1)
        if t < F - 1:
            gather_step(t)
        if t + 1 < G:
            send_chunk(t + 1)
    for c in range(max(F - 1, 3) + 1, G):
        send_chunk(c)

    for copy in local[1:4]:
        copy.wait()
    for o in range(1, G):
        for copy in s_in(o):
            copy.wait_recv()

    block = (G, F, pix, HDIM)

    @pl.loop(0, HC)
    def _(h):
        at = hcols(h)
        q, k, v = (flat(srecv[i, :, :, :, at]) for i in range(3))
        gr = live_rows(flat(srecv[3, :, :, :, at]), f * (G * T))
        out, dq, dk, dv = many(k, v, q, gr, G * T, None)
        sres[0, :, :, :, at] = unflat(out, block)
        sres[1, :, :, :, at] = unflat(dq, block)
        sres[2, :, :, :, at] = unflat(dk, block)
        sres[3, :, :, :, at] = unflat(dv, block)

    def sb_grads(o, i, src_i):
        return remote(sres.at[pl.ds(1, 3), i], sgrad.at[:, :, :, cols(src_i)], sb_s.at[o, 0], sb_r.at[o, 0], at_mate(i))

    def sb_cross(o, i, src_i):
        return (
            remote(sres.at[0, i], spo.at[:, :, cols(src_i)], sb_s.at[o, 1], sb_r.at[o, 1], at_mate(i)),
            remote(sres.at[4, i], cqgrad.at[:, :, cols(src_i)], sb_s.at[o, 2], sb_r.at[o, 2], at_mate(i)),
        )

    for o in range(1, G):
        sb_grads(o, mate(o), g).start()
    home.append(pltpu.make_async_copy(sres.at[pl.ds(1, 3), g], sgrad.at[:, :, :, cols(g)], loc.at[0]))
    home[-1].start()

    @pl.when(f == F - 1)
    def _():
        up(0).wait_recv()

    @pl.when(f == 0)
    def _():
        down(F - 1).wait_recv()

    @pl.loop(0, S)
    def _(s):
        at = pl.ds(pl.multiple_of(s * RP, 8), R)
        for i in range(2):
            cf[i, at, :] = crecv[s, i].astype(F32)
        ids = s * R + lax.broadcasted_iota(jnp.int32, (R, HDIM), 0)
        cbias[at, :] = jnp.where(ids < clen, 0.0, LOW)

    ckv[...] = cf[...].astype(BF16)

    @pl.loop(0, HC)
    def _(h):
        at = hcols(h)
        q = flat(srecv[4, :, :, :, at])
        gr = live_rows(flat(srecv[3, :, :, :, at]), f * (G * T))
        k = ckv[0, :, at]
        v = ckv[1, :, at]
        out, dq, dk, dv = many(k, v, q, gr, KP, cbias[...])
        total = flat(sres[0, :, :, :, at]).astype(F32) + out
        sres[0, :, :, :, at] = unflat(total, block)
        sres[4, :, :, :, at] = unflat(dq, block)
        cacc[0, :, at] = dk
        cacc[1, :, at] = dv

    @pl.loop(0, S)
    def _(s):
        at = pl.ds(pl.multiple_of(s * RP, 8), R)
        for i in range(2):
            cg[s, i] = cacc[i, at, :].astype(BF16)

    def c3_up(j):
        return remote(cg.at[piece(j)], cgu.at[j], c3_s.at[0, j], c3_r.at[0, j], at_line(line(1)))

    def c3_down(j):
        return remote(cg.at[piece(j)], cgd.at[j], c3_s.at[1, j], c3_r.at[1, j], at_line(line_from(1)))

    def reduce_step(t):
        def hop(j, send, arrived):
            if t > 0:
                send.wait_recv()
                cg[piece(j)] = (cg[piece(j)].astype(F32) + arrived[j].astype(F32)).astype(BF16)
            send.start()

        @pl.when(f == t)
        def _():
            @pl.loop(0, F - 1 - t)
            def _(i):
                j = F - 1 - i
                hop(j, c3_up(j), cgu)

        @pl.when(f == F - 1 - t)
        def _():
            @pl.loop(0, F - 1 - t)
            def _(j):
                hop(j, c3_down(j), cgd)

    reduce_step(0)
    for o in range(1, G):
        for copy in sb_cross(o, mate(o), g):
            copy.start()
    home.append(pltpu.make_async_copy(sres.at[0, g], spo.at[:, :, cols(g)], loc.at[1]))
    home.append(pltpu.make_async_copy(sres.at[4, g], cqgrad.at[:, :, cols(g)], loc.at[2]))
    home[-2].start()
    home[-1].start()

    for t in range(1, max(F - 1, G - 1)):
        if t + 1 < G:
            temporal_chunk(t + 1)
            temporal_home(t + 1)
        if t < F - 1:
            reduce_step(t)

    for i in range(G):
        at = pl.ds(pl.multiple_of((f * G + i) * RP, 8), R)
        for b in range(2):
            fin[i, b] = cacc[b, at, :]

    @pl.when(f > 0)
    def _():
        c3_up(f).wait_recv()
        fin[...] += cgu[f].astype(F32)

    @pl.when(f < F - 1)
    def _():
        c3_down(f).wait_recv()
        fin[...] += cgd[f].astype(F32)

    def c4(o, i, src_i):
        return remote(fin.at[i], capgrad.at[:, :, cols(src_i)], c4_s.at[o], c4_r.at[o], at_mate(i))

    for o in range(1, G):
        c4(o, mate(o), g).start()
    home.append(pltpu.make_async_copy(fin.at[g], capgrad.at[:, :, cols(g)], loc.at[3]))
    home[-1].start()

    for o in range(1, G):
        i = mate_from(o)
        sb_grads(o, i, i).wait_recv()
        for copy in sb_cross(o, i, i):
            copy.wait_recv()
    for copy in home:
        copy.wait()

    @pl.loop(0, G)
    def _(c):
        for o in range(1, F):
            j = line_from(o)
            for copy in tb(c, o, j, j):
                copy.wait_recv()

    shape3 = (F, pix, W)
    tok = (
        dev * T
        + lax.broadcasted_iota(jnp.int32, shape3, 0) * pix
        + lax.broadcasted_iota(jnp.int32, shape3, 1)
    )
    for c in range(G):
        at = slice(c * W, (c + 1) * W)
        total = spo[:, :, at].astype(F32) + tmo[:, :, at].astype(F32)
        mixed[:, :, at] = jnp.where(tok < live, total, 0.0).astype(BF16)

    for o in range(1, G):
        i = mate_from(o)
        c4(o, i, i).wait_recv()

    for o in range(1, G):
        c1(o).wait_send()
        for copy in s_out(o):
            copy.wait_send()
        sb_grads(o, mate(o), g).wait_send()
        for copy in sb_cross(o, mate(o), g):
            copy.wait_send()
        c4(o, mate(o), g).wait_send()

    @pl.when(f < F - 1)
    def _():
        @pl.loop(0, F)
        def _(i):
            @pl.when(i <= f)
            def _():
                up(i).wait_send()

            @pl.when(i > f)
            def _():
                c3_up(i).wait_send()

    @pl.when(f > 0)
    def _():
        @pl.loop(0, F)
        def _(i):
            @pl.when(i >= f)
            def _():
                down(i).wait_send()

            @pl.when(i < f)
            def _():
                c3_down(i).wait_send()

    @pl.loop(0, G)
    def _(c):
        for o in range(1, F):
            for copy in t_out(c, o):
                copy.wait_send()
            for copy in tb(c, o, line(o), f):
                copy.wait_send()


def hand_on(*refs):
    n = 4
    srcs, caps, dsts, capo = refs[:n], refs[n], refs[n + 1 : 2 * n + 1], refs[2 * n + 1]
    holds, sem_in, sem_out = refs[2 * n + 2 : 3 * n + 2], refs[-2], refs[-1]
    pieces = []
    for src, hold, dst in zip(srcs, holds, dsts):
        if src.ndim == 3:
            pieces += [(src.at[i], hold.at[i], dst.at[i]) for i in range(src.shape[0])]
        else:
            half = src.shape[0] // 2
            pieces += [tuple(r.at[pl.ds(i * half, half)] for r in (src, hold, dst)) for i in range(2)]
    take = [pltpu.make_async_copy(a, b, sem_in.at[i]) for i, (a, b, _) in enumerate(pieces)]
    give = [pltpu.make_async_copy(b, c, sem_out.at[i]) for i, (_, b, c) in enumerate(pieces)]
    for copy in take:
        copy.start()
    for i in range(2):
        capo[:, i, :] = caps[i]
    for first, second in zip(take, give):
        first.wait()
        second.start()
    for copy in give:
        copy.wait()


def local(spatial_qkv, temporal_qkv, cross_query, caption_kv, out_grad, live_tokens, caption_len):
    devices = lax.axis_size("seq")
    rows, width = out_grad.shape
    G = P_SIZE // rows
    F = devices // G
    pix = rows // F
    W = width // G
    HC = W // HDIM
    R = caption_kv.shape[0]
    RP = (R + 7) // 8 * 8
    S = G * F
    KP = S * RP
    keys = max(KP, G * rows)
    geo = (G, F, pix, W, HC, R, RP)
    dma = pltpu.SemaphoreType.DMA
    any_spec = pl.BlockSpec(memory_space=pl.ANY)
    smem = pl.BlockSpec(memory_space=pltpu.SMEM)
    vmem = pl.BlockSpec(memory_space=pltpu.VMEM)
    mixed, sgrad, tgrad, cqgrad, capgrad = pl.pallas_call(
        functools.partial(kernel, geo),
        out_shape=(
            jax.ShapeDtypeStruct((F, pix, width), BF16),
            jax.ShapeDtypeStruct((3, F, pix, width), BF16),
            jax.ShapeDtypeStruct((3, F, pix, width), BF16),
            jax.ShapeDtypeStruct((F, pix, width), BF16),
            jax.ShapeDtypeStruct((2, R, width), F32),
        ),
        in_specs=[smem, smem, any_spec, any_spec, any_spec, vmem, any_spec],
        out_specs=(vmem, any_spec, any_spec, any_spec, any_spec),
        scratch_shapes=[
            pltpu.VMEM((5, G, F, pix, W), BF16),
            pltpu.VMEM((5, G, F, pix, W), BF16),
            pltpu.VMEM((G, 4, F, pix, W), BF16),
            pltpu.VMEM((G, 4, F, pix, W), BF16),
            pltpu.VMEM((S, 2, R, W), BF16),
            pltpu.VMEM((2, KP, W), F32),
            pltpu.VMEM((2, KP, W), BF16),
            pltpu.VMEM((KP, HDIM), F32),
            pltpu.VMEM((2, KP, W), F32),
            pltpu.VMEM((S, 2, R, W), BF16),
            pltpu.VMEM((F, G, 2, R, W), BF16),
            pltpu.VMEM((F, G, 2, R, W), BF16),
            pltpu.VMEM((G, 2, R, W), F32),
            pltpu.VMEM((F, pix, width), BF16),
            pltpu.VMEM((F, pix, width), BF16),
            pltpu.VMEM((keys, G * rows), BF16),
            pltpu.VMEM((keys, G * rows), BF16),
            pltpu.VMEM((rows, rows), F32),
            pltpu.VMEM((2, R, width), BF16),
            dma((4 + 2 * G,)),
            dma((G, F, 2)), dma((G, F, 2)),
            dma((G, F, 2)), dma((G, F, 2)),
            dma((G, 3)), dma((G, 3)),
            dma((G, 3)), dma((G, 3)),
            dma((G,)), dma((G,)),
            dma((2, F)), dma((2, F)),
            dma((2, F)), dma((2, F)),
            dma((G,)), dma((G,)),
        ],
        compiler_params=pltpu.CompilerParams(
            collective_id=0, has_side_effects=True, vmem_limit_bytes=60 * 1024 * 1024
        ),
    )(
        live_tokens,
        caption_len,
        spatial_qkv.reshape(3, F, pix, width),
        temporal_qkv.reshape(3, F, pix, width),
        cross_query.reshape(F, pix, width),
        caption_kv,
        out_grad.reshape(F, pix, width),
    )
    return pl.pallas_call(
        hand_on,
        out_shape=(
            jax.ShapeDtypeStruct((rows, width), BF16),
            jax.ShapeDtypeStruct((3, rows, width), BF16),
            jax.ShapeDtypeStruct((3, rows, width), BF16),
            jax.ShapeDtypeStruct((rows, width), BF16),
            jax.ShapeDtypeStruct((R, 2, width), F32),
        ),
        in_specs=[any_spec] * 4 + [vmem],
        out_specs=(any_spec, any_spec, any_spec, any_spec, vmem),
        scratch_shapes=[
            pltpu.VMEM((rows, width), BF16),
            pltpu.VMEM((3, rows, width), BF16),
            pltpu.VMEM((3, rows, width), BF16),
            pltpu.VMEM((rows, width), BF16),
            dma((10,)),
            dma((10,)),
        ],
        compiler_params=pltpu.CompilerParams(vmem_limit_bytes=60 * 1024 * 1024),
    )(
        mixed.reshape(rows, width),
        sgrad.reshape(3, rows, width),
        tgrad.reshape(3, rows, width),
        cqgrad.reshape(rows, width),
        capgrad,
    )


def solution(mesh):
    placed = (
        P(None, ("dp", "seq"), None),
        P(None, ("dp", "seq"), None),
        P(("dp", "seq"), None),
        P(("dp", "seq"), None, None),
        P(("dp", "seq"), None),
        P("dp"),
        P("dp"),
    )
    return jax.shard_map(
        local,
        mesh=mesh,
        in_specs=placed,
        out_specs=(
            P(("dp", "seq"), None),
            P(None, ("dp", "seq"), None),
            P(None, ("dp", "seq"), None),
            P(("dp", "seq"), None),
            P(("dp", "seq"), None, None),
        ),
        check_vma=False,
    )
```

```python
import functools

import jax
import jax.numpy as jnp
from jax import lax
from jax.experimental import pallas as pl
from jax.experimental.pallas import tpu as pltpu
from jax.sharding import PartitionSpec as P

HDIM = 128
P_SIZE = 512
F32 = jnp.float32
BF16 = jnp.bfloat16
LOW = -1e30


def dot_nt(a, b):
    return lax.dot_general(a, b, (((1,), (1,)), ((), ())), preferred_element_type=F32)


def dot_tn(a, b):
    return lax.dot_general(a, b, (((0,), (0,)), ((), ())), preferred_element_type=F32)


def dot_nn(a, b):
    return lax.dot_general(a, b, (((1,), (0,)), ((), ())), preferred_element_type=F32)


def flat(x):
    rows = 1
    for n in x.shape[:-1]:
        rows *= n
    if x.shape[-2] % 16:
        return x.astype(F32).reshape(rows, x.shape[-1]).astype(BF16)
    return x.reshape(rows, x.shape[-1])


def unflat(x, shape):
    if shape[-2] % 16:
        return x.reshape(shape).astype(BF16)
    return x.astype(BF16).reshape(shape)


def slopes(q, k, v, g, scale, bias):
    s = dot_nt(k, q) * scale
    if bias is not None:
        s = s + bias
    p = jnp.exp(s - jnp.max(s, axis=0, keepdims=True))
    w = p * (1.0 / jnp.sum(p, axis=0, keepdims=True))
    dp = dot_nt(v, g)
    delta = jnp.sum(w * dp, axis=0, keepdims=True)
    return w.astype(BF16), (w * (dp - delta)).astype(BF16)


def kernel(
    geo,
    live_ref, clen_ref, sqkv, tqkv, cq, cap_in, og,
    mixed, sgrad, tgrad, cqgrad, capgrad,
    srecv, sres, trecv, tres, crecv, cf, ckv, cbias, cacc, cg, cgu, cgd, fin, spo, tmo, wbuf, dbuf, tbias, cap, cap_rows, mix,
    loc, t_s, t_r, tb_s, tb_r, s_s, s_r, sb_s, sb_r, c1_s, c1_r, c2_s, c2_r, c3_s, c3_r, c4_s, c4_r,
):
    G, F, pix, W, HC, R, RP = geo
    S = G * F
    KP = S * RP
    T = F * pix
    scale = HDIM ** (-0.5)
    dev = lax.axis_index("seq")
    f = dev // G
    g = dev % G
    live = live_ref[0]
    clen = clen_ref[0]

    def cols(i):
        return pl.ds(pl.multiple_of(i * W, 128), W)

    def hcols(h):
        return pl.ds(pl.multiple_of(h * HDIM, 128), HDIM)

    def mate(o):
        return (g + o) % G

    def mate_from(o):
        return (g + G - o) % G

    def line(o):
        return (f + o) % F

    def line_from(o):
        return (f + F - o) % F

    def at_mate(i):
        return f * G + i

    def at_line(i):
        return i * G + g

    def remote(src, dst, ss, rs, to):
        return pltpu.make_async_remote_copy(
            src_ref=src, dst_ref=dst, send_sem=ss, recv_sem=rs,
            device_id={"seq": to}, device_id_type=pl.DeviceIdType.MESH,
        )

    cap_copy = pltpu.make_async_copy(cap_in, cap_rows, loc.at[0])
    cap_copy.start()
    barrier = pltpu.get_barrier_semaphore()
    for o in range(1, G):
        pl.semaphore_signal(barrier, inc=1, device_id={"seq": at_mate(mate(o))}, device_id_type=pl.DeviceIdType.MESH)
    for o in range(1, F):
        pl.semaphore_signal(barrier, inc=1, device_id={"seq": at_line(line(o))}, device_id_type=pl.DeviceIdType.MESH)

    local = [
        pltpu.make_async_copy(cap.at[:, :, cols(g)], crecv.at[dev], loc.at[0]),
        pltpu.make_async_copy(sqkv.at[:, :, :, cols(g)], srecv.at[pl.ds(0, 3), g], loc.at[1]),
        pltpu.make_async_copy(og.at[:, :, cols(g)], srecv.at[3, g], loc.at[2]),
        pltpu.make_async_copy(cq.at[:, :, cols(g)], srecv.at[4, g], loc.at[3]),
    ]
    for c in range(G):
        local.append(pltpu.make_async_copy(tqkv.at[:, f, :, cols(c)], trecv.at[c, pl.ds(0, 3), f], loc.at[4 + 2 * c]))
        local.append(pltpu.make_async_copy(og.at[f, :, cols(c)], trecv.at[c, 3, f], loc.at[5 + 2 * c]))
    cap_copy.wait()
    for i in range(2):
        cap[i] = cap_rows[:, i, :]
    pl.semaphore_wait(barrier, G + F - 2)

    def c1(o):
        return remote(cap.at[:, :, cols(mate(o))], crecv.at[dev], c1_s.at[o], c1_r.at[o], at_mate(mate(o)))

    def c1_in(o):
        i = mate_from(o)
        return remote(cap.at[:, :, cols(i)], crecv.at[at_mate(i)], c1_s.at[o], c1_r.at[o], at_mate(i))

    def t_out(c, o):
        j = line(o)
        return (
            remote(tqkv.at[:, j, :, cols(c)], trecv.at[c, pl.ds(0, 3), f], t_s.at[c, o, 0], t_r.at[c, o, 0], at_line(j)),
            remote(og.at[j, :, cols(c)], trecv.at[c, 3, f], t_s.at[c, o, 1], t_r.at[c, o, 1], at_line(j)),
        )

    def t_in(c, o):
        j = line_from(o)
        return (
            remote(tqkv.at[:, j, :, cols(c)], trecv.at[c, pl.ds(0, 3), j], t_s.at[c, o, 0], t_r.at[c, o, 0], at_line(j)),
            remote(og.at[j, :, cols(c)], trecv.at[c, 3, j], t_s.at[c, o, 1], t_r.at[c, o, 1], at_line(j)),
        )

    def s_out(o):
        i = mate(o)
        return (
            remote(sqkv.at[:, :, :, cols(i)], srecv.at[pl.ds(0, 3), g], s_s.at[o, 0], s_r.at[o, 0], at_mate(i)),
            remote(og.at[:, :, cols(i)], srecv.at[3, g], s_s.at[o, 1], s_r.at[o, 1], at_mate(i)),
            remote(cq.at[:, :, cols(i)], srecv.at[4, g], s_s.at[o, 2], s_r.at[o, 2], at_mate(i)),
        )

    def s_in(o):
        i = mate_from(o)
        return (
            remote(sqkv.at[:, :, :, cols(i)], srecv.at[pl.ds(0, 3), i], s_s.at[o, 0], s_r.at[o, 0], at_mate(i)),
            remote(og.at[:, :, cols(i)], srecv.at[3, i], s_s.at[o, 1], s_r.at[o, 1], at_mate(i)),
            remote(cq.at[:, :, cols(i)], srecv.at[4, i], s_s.at[o, 2], s_r.at[o, 2], at_mate(i)),
        )

    def send_chunk(c):
        for o in range(1, F):
            for copy in t_out(c, o):
                copy.start()

    for o in range(1, G):
        c1(o).start()
    send_chunk(0)
    for o in range(1, G):
        for copy in s_out(o):
            copy.start()

    def piece(i):
        return pl.ds(i * G, G)

    def up(i):
        return remote(crecv.at[piece(i)], crecv.at[piece(i)], c2_s.at[0, i], c2_r.at[0, i], at_line(line(1)))

    def down(i):
        return remote(crecv.at[piece(i)], crecv.at[piece(i)], c2_s.at[1, i], c2_r.at[1, i], at_line(line_from(1)))

    def gather_step(t):
        @pl.when(f >= t)
        def _():
            if t > 0:
                up(f - t).wait_recv()

            @pl.when(f < F - 1)
            def _():
                up(f - t).start()

        @pl.when(f + t < F)
        def _():
            if t > 0:
                down(f + t).wait_recv()

            @pl.when(f > 0)
            def _():
                down(f + t).start()

    for copy in local:
        copy.start()
    local[0].wait()
    for o in range(1, G):
        c1_in(o).wait_recv()
    gather_step(0)
    if F > 2:
        gather_step(1)
    send_chunk(1)

    cf[...] = jnp.zeros(cf.shape, F32)
    cbias[...] = jnp.full(cbias.shape, LOW, F32)

    def live_rows(x, first):
        ids = first + lax.broadcasted_iota(jnp.int32, x.shape, 0)
        return jnp.where(ids < live, x.astype(F32), 0.0).astype(BF16)

    def many(k, v, q, gr, keys, bias):
        for b in range(G):
            rows = slice(b * T, (b + 1) * T)
            w, d = slopes(q[rows], k, v, gr[rows], scale, bias)
            wbuf[pl.ds(0, keys), rows] = w
            dbuf[pl.ds(0, keys), rows] = d
        w = wbuf[pl.ds(0, keys), :]
        d = dbuf[pl.ds(0, keys), :]
        return dot_tn(w, v), dot_tn(d, k) * scale, dot_nn(d, q) * scale, dot_nn(w, gr)

    rk = lax.broadcasted_iota(jnp.int32, (T, T), 0)
    rq = lax.broadcasted_iota(jnp.int32, (T, T), 1)
    shift = pix.bit_length() - 1
    first = g * T + f * pix
    key_token = (rk >> shift) * P_SIZE + (rk & (pix - 1)) + first
    same = ((rk & (pix - 1)) == (rq & (pix - 1))) & (key_token < live)
    tbias[...] = jnp.where(same, 0.0, LOW)

    def tb(c, o, j, src_j):
        return (
            remote(tres.at[c, 0, j], tmo.at[src_j, :, cols(c)], tb_s.at[c, o, 0], tb_r.at[c, o, 0], at_line(j)),
            remote(tres.at[c, pl.ds(1, 3), j], tgrad.at[:, src_j, :, cols(c)], tb_s.at[c, o, 1], tb_r.at[c, o, 1], at_line(j)),
        )

    tblock = (F, pix, HDIM)
    home = []

    def temporal_chunk(c):
        for o in range(1, F):
            for copy in t_in(c, o):
                copy.wait_recv()
        rd = lax.broadcasted_iota(jnp.int32, (T, HDIM), 0)
        t_live = ((rd >> shift) * P_SIZE + (rd & (pix - 1)) + first) < live
        for h in range(HC):
            at = pl.ds(h * HDIM, HDIM)
            q, k, v, gr = (flat(trecv[c, i, :, :, at]) for i in range(4))
            gr = jnp.where(t_live, gr.astype(F32), 0.0).astype(BF16)
            w, d = slopes(q, k, v, gr, scale, tbias[...])
            tres[c, 0, :, :, at] = unflat(dot_tn(w, v), tblock)
            tres[c, 1, :, :, at] = unflat(dot_tn(d, k) * scale, tblock)
            tres[c, 2, :, :, at] = unflat(dot_nn(d, q) * scale, tblock)
            tres[c, 3, :, :, at] = unflat(dot_nn(w, gr), tblock)
        for o in range(1, F):
            for copy in tb(c, o, line(o), f):
                copy.start()

    def temporal_home(c):
        mine = [
            pltpu.make_async_copy(tres.at[c, 0, f], tmo.at[f, :, cols(c)], loc.at[4 + 2 * c]),
            pltpu.make_async_copy(tres.at[c, pl.ds(1, 3), f], tgrad.at[:, f, :, cols(c)], loc.at[5 + 2 * c]),
        ]
        for copy in mine:
            copy.start()
        home.extend(mine)

    for c in range(G):
        local[4 + 2 * c].wait()
        local[5 + 2 * c].wait()
    for t in range(1, max(F - 1, 3)):
        if t <= 2:
            temporal_chunk(t - 1)
            temporal_home(t - 1)
        if t + 1 < F - 1:
            gather_step(t + 1)
        if t + 1 < G:
            send_chunk(t + 1)
    for c in range(max(F - 1, 3) + 1, G):
        send_chunk(c)

    for copy in local[1:4]:
        copy.wait()
    for o in range(1, G):
        for copy in s_in(o):
            copy.wait_recv()

    block = (G, F, pix, HDIM)

    @pl.loop(0, HC)
    def _(h):
        at = hcols(h)
        q, k, v = (flat(srecv[i, :, :, :, at]) for i in range(3))
        gr = live_rows(flat(srecv[3, :, :, :, at]), f * (G * T))
        out, dq, dk, dv = many(k, v, q, gr, G * T, None)
        sres[0, :, :, :, at] = unflat(out, block)
        sres[1, :, :, :, at] = unflat(dq, block)
        sres[2, :, :, :, at] = unflat(dk, block)
        sres[3, :, :, :, at] = unflat(dv, block)

    def sb_grads(o, i, src_i):
        return remote(sres.at[pl.ds(1, 3), i], sgrad.at[:, :, :, cols(src_i)], sb_s.at[o, 0], sb_r.at[o, 0], at_mate(i))

    def sb_cross(o, i, src_i):
        return (
            remote(sres.at[0, i], spo.at[:, :, cols(src_i)], sb_s.at[o, 1], sb_r.at[o, 1], at_mate(i)),
            remote(sres.at[4, i], cqgrad.at[:, :, cols(src_i)], sb_s.at[o, 2], sb_r.at[o, 2], at_mate(i)),
        )

    for o in range(1, G):
        sb_grads(o, mate(o), g).start()
    home.append(pltpu.make_async_copy(sres.at[pl.ds(1, 3), g], sgrad.at[:, :, :, cols(g)], loc.at[0]))
    home[-1].start()

    @pl.when(f == F - 1)
    def _():
        up(0).wait_recv()

    @pl.when(f == 0)
    def _():
        down(F - 1).wait_recv()

    @pl.loop(0, S)
    def _(s):
        at = pl.ds(pl.multiple_of(s * RP, 8), R)
        for i in range(2):
            cf[i, at, :] = crecv[s, i].astype(F32)
        ids = s * R + lax.broadcasted_iota(jnp.int32, (R, HDIM), 0)
        cbias[at, :] = jnp.where(ids < clen, 0.0, LOW)

    ckv[...] = cf[...].astype(BF16)

    @pl.loop(0, HC)
    def _(h):
        at = hcols(h)
        q = flat(srecv[4, :, :, :, at])
        gr = live_rows(flat(srecv[3, :, :, :, at]), f * (G * T))
        k = ckv[0, :, at]
        v = ckv[1, :, at]
        out, dq, dk, dv = many(k, v, q, gr, KP, cbias[...])
        total = flat(sres[0, :, :, :, at]).astype(F32) + out
        sres[0, :, :, :, at] = unflat(total, block)
        sres[4, :, :, :, at] = unflat(dq, block)
        cacc[0, :, at] = dk
        cacc[1, :, at] = dv

    @pl.loop(0, S)
    def _(s):
        at = pl.ds(pl.multiple_of(s * RP, 8), R)
        for i in range(2):
            cg[s, i] = cacc[i, at, :].astype(BF16)

    def c3_up(j):
        return remote(cg.at[piece(j)], cgu.at[j], c3_s.at[0, j], c3_r.at[0, j], at_line(line(1)))

    def c3_down(j):
        return remote(cg.at[piece(j)], cgd.at[j], c3_s.at[1, j], c3_r.at[1, j], at_line(line_from(1)))

    def reduce_step(t):
        def hop(j, send, arrived):
            if t > 0:
                send.wait_recv()
                cg[piece(j)] = (cg[piece(j)].astype(F32) + arrived[j].astype(F32)).astype(BF16)
            send.start()

        @pl.when(f == t)
        def _():
            @pl.loop(0, F - 1 - t)
            def _(i):
                j = F - 1 - i
                hop(j, c3_up(j), cgu)

        @pl.when(f == F - 1 - t)
        def _():
            @pl.loop(0, F - 1 - t)
            def _(j):
                hop(j, c3_down(j), cgd)

    reduce_step(0)
    for o in range(1, G):
        for copy in sb_cross(o, mate(o), g):
            copy.start()
    home.append(pltpu.make_async_copy(sres.at[0, g], spo.at[:, :, cols(g)], loc.at[1]))
    home.append(pltpu.make_async_copy(sres.at[4, g], cqgrad.at[:, :, cols(g)], loc.at[2]))
    home[-2].start()
    home[-1].start()

    for t in range(1, max(F - 1, G - 1)):
        if t + 1 < G:
            temporal_chunk(t + 1)
            temporal_home(t + 1)
        if t < F - 1:
            reduce_step(t)

    for i in range(G):
        at = pl.ds(pl.multiple_of((f * G + i) * RP, 8), R)
        for b in range(2):
            fin[i, b] = cacc[b, at, :]

    @pl.when(f > 0)
    def _():
        c3_up(f).wait_recv()
        fin[...] += cgu[f].astype(F32)

    @pl.when(f < F - 1)
    def _():
        c3_down(f).wait_recv()
        fin[...] += cgd[f].astype(F32)

    def c4(o, i, src_i):
        return remote(fin.at[i], capgrad.at[:, :, cols(src_i)], c4_s.at[o], c4_r.at[o], at_mate(i))

    for o in range(1, G):
        c4(o, mate(o), g).start()
    home.append(pltpu.make_async_copy(fin.at[g], capgrad.at[:, :, cols(g)], loc.at[3]))
    home[-1].start()

    for o in range(1, G):
        i = mate_from(o)
        sb_grads(o, i, i).wait_recv()
        for copy in sb_cross(o, i, i):
            copy.wait_recv()
    for copy in home:
        copy.wait()

    @pl.loop(0, G)
    def _(c):
        for o in range(1, F):
            j = line_from(o)
            for copy in tb(c, o, j, j):
                copy.wait_recv()

    mixed_out = []
    shape3 = (F, pix, W)
    tok = (
        dev * T
        + lax.broadcasted_iota(jnp.int32, shape3, 0) * pix
        + lax.broadcasted_iota(jnp.int32, shape3, 1)
    )
    for c in range(G):
        at = slice(c * W, (c + 1) * W)
        total = spo[:, :, at].astype(F32) + tmo[:, :, at].astype(F32)
        mix[:, :, at] = jnp.where(tok < live, total, 0.0).astype(BF16)
        out = pltpu.make_async_copy(mix.at[:, :, pl.ds(c * W, W)], mixed.at[:, :, pl.ds(c * W, W)], loc.at[4 + 2 * c])
        out.start()
        mixed_out.append(out)

    for o in range(1, G):
        i = mate_from(o)
        c4(o, i, i).wait_recv()

    for copy in mixed_out:
        copy.wait()

    for o in range(1, G):
        c1(o).wait_send()
        for copy in s_out(o):
            copy.wait_send()
        sb_grads(o, mate(o), g).wait_send()
        for copy in sb_cross(o, mate(o), g):
            copy.wait_send()
        c4(o, mate(o), g).wait_send()

    @pl.when(f < F - 1)
    def _():
        @pl.loop(0, F)
        def _(i):
            @pl.when(i <= f)
            def _():
                up(i).wait_send()

            @pl.when(i > f)
            def _():
                c3_up(i).wait_send()

    @pl.when(f > 0)
    def _():
        @pl.loop(0, F)
        def _(i):
            @pl.when(i >= f)
            def _():
                down(i).wait_send()

            @pl.when(i < f)
            def _():
                c3_down(i).wait_send()

    @pl.loop(0, G)
    def _(c):
        for o in range(1, F):
            for copy in t_out(c, o):
                copy.wait_send()
            for copy in tb(c, o, line(o), f):
                copy.wait_send()


def hand_on(*refs):
    n = 4
    srcs, caps, dsts, capo = refs[:n], refs[n], refs[n + 1 : 2 * n + 1], refs[2 * n + 1]
    holds, (cap_in, cap_out, sem_in, sem_out) = refs[2 * n + 2 : 3 * n + 2], refs[3 * n + 2 :]
    pieces = []
    for src, hold, dst in zip(srcs, holds, dsts):
        if src.ndim == 3:
            pieces += [(src.at[i], hold.at[i], dst.at[i]) for i in range(src.shape[0])]
        else:
            half = src.shape[0] // 2
            pieces += [tuple(r.at[pl.ds(i * half, half)] for r in (src, hold, dst)) for i in range(2)]
    take = [pltpu.make_async_copy(a, b, sem_in.at[i]) for i, (a, b, _) in enumerate(pieces)]
    give = [pltpu.make_async_copy(b, c, sem_out.at[i]) for i, (_, b, c) in enumerate(pieces)]
    cap_take = pltpu.make_async_copy(caps, cap_in, sem_in.at[10])
    cap_take.start()
    for copy in take:
        copy.start()
    for first, second in zip(take, give):
        first.wait()
        second.start()
    cap_take.wait()
    for i in range(2):
        cap_out[:, i, :] = cap_in[i]
    give.append(pltpu.make_async_copy(cap_out, capo, sem_out.at[10]))
    give[-1].start()
    for copy in give:
        copy.wait()


def local(spatial_qkv, temporal_qkv, cross_query, caption_kv, out_grad, live_tokens, caption_len):
    devices = lax.axis_size("seq")
    rows, width = out_grad.shape
    G = P_SIZE // rows
    F = devices // G
    pix = rows // F
    W = width // G
    HC = W // HDIM
    R = caption_kv.shape[0]
    RP = (R + 7) // 8 * 8
    S = G * F
    KP = S * RP
    keys = max(KP, G * rows)
    geo = (G, F, pix, W, HC, R, RP)
    dma = pltpu.SemaphoreType.DMA
    any_spec = pl.BlockSpec(memory_space=pl.ANY)
    smem = pl.BlockSpec(memory_space=pltpu.SMEM)
    mixed, sgrad, tgrad, cqgrad, capgrad = pl.pallas_call(
        functools.partial(kernel, geo),
        out_shape=(
            jax.ShapeDtypeStruct((F, pix, width), BF16),
            jax.ShapeDtypeStruct((3, F, pix, width), BF16),
            jax.ShapeDtypeStruct((3, F, pix, width), BF16),
            jax.ShapeDtypeStruct((F, pix, width), BF16),
            jax.ShapeDtypeStruct((2, R, width), F32),
        ),
        in_specs=[smem, smem] + [any_spec] * 5,
        out_specs=(any_spec,) * 5,
        scratch_shapes=[
            pltpu.VMEM((5, G, F, pix, W), BF16),
            pltpu.VMEM((5, G, F, pix, W), BF16),
            pltpu.VMEM((G, 4, F, pix, W), BF16),
            pltpu.VMEM((G, 4, F, pix, W), BF16),
            pltpu.VMEM((S, 2, R, W), BF16),
            pltpu.VMEM((2, KP, W), F32),
            pltpu.VMEM((2, KP, W), BF16),
            pltpu.VMEM((KP, HDIM), F32),
            pltpu.VMEM((2, KP, W), F32),
            pltpu.VMEM((S, 2, R, W), BF16),
            pltpu.VMEM((F, G, 2, R, W), BF16),
            pltpu.VMEM((F, G, 2, R, W), BF16),
            pltpu.VMEM((G, 2, R, W), F32),
            pltpu.VMEM((F, pix, width), BF16),
            pltpu.VMEM((F, pix, width), BF16),
            pltpu.VMEM((keys, G * rows), BF16),
            pltpu.VMEM((keys, G * rows), BF16),
            pltpu.VMEM((rows, rows), F32),
            pltpu.VMEM((2, R, width), BF16),
            pltpu.VMEM((R, 2, width), BF16),
            pltpu.VMEM((F, pix, width), BF16),
            dma((4 + 2 * G,)),
            dma((G, F, 2)), dma((G, F, 2)),
            dma((G, F, 2)), dma((G, F, 2)),
            dma((G, 3)), dma((G, 3)),
            dma((G, 3)), dma((G, 3)),
            dma((G,)), dma((G,)),
            dma((2, F)), dma((2, F)),
            dma((2, F)), dma((2, F)),
            dma((G,)), dma((G,)),
        ],
        compiler_params=pltpu.CompilerParams(
            collective_id=0, has_side_effects=True, vmem_limit_bytes=60 * 1024 * 1024
        ),
    )(
        live_tokens,
        caption_len,
        spatial_qkv.reshape(3, F, pix, width),
        temporal_qkv.reshape(3, F, pix, width),
        cross_query.reshape(F, pix, width),
        caption_kv,
        out_grad.reshape(F, pix, width),
    )
    return pl.pallas_call(
        hand_on,
        out_shape=(
            jax.ShapeDtypeStruct((rows, width), BF16),
            jax.ShapeDtypeStruct((3, rows, width), BF16),
            jax.ShapeDtypeStruct((3, rows, width), BF16),
            jax.ShapeDtypeStruct((rows, width), BF16),
            jax.ShapeDtypeStruct((R, 2, width), F32),
        ),
        in_specs=[any_spec] * 5,
        out_specs=(any_spec,) * 5,
        scratch_shapes=[
            pltpu.VMEM((rows, width), BF16),
            pltpu.VMEM((3, rows, width), BF16),
            pltpu.VMEM((3, rows, width), BF16),
            pltpu.VMEM((rows, width), BF16),
            pltpu.VMEM((2, R, width), F32),
            pltpu.VMEM((R, 2, width), F32),
            dma((11,)),
            dma((11,)),
        ],
        compiler_params=pltpu.CompilerParams(vmem_limit_bytes=60 * 1024 * 1024),
    )(
        mixed.reshape(rows, width),
        sgrad.reshape(3, rows, width),
        tgrad.reshape(3, rows, width),
        cqgrad.reshape(rows, width),
        capgrad,
    )


def solution(mesh):
    placed = (
        P(None, ("dp", "seq"), None),
        P(None, ("dp", "seq"), None),
        P(("dp", "seq"), None),
        P(("dp", "seq"), None, None),
        P(("dp", "seq"), None),
        P("dp"),
        P("dp"),
    )
    return jax.shard_map(
        local,
        mesh=mesh,
        in_specs=placed,
        out_specs=(
            P(("dp", "seq"), None),
            P(None, ("dp", "seq"), None),
            P(None, ("dp", "seq"), None),
            P(("dp", "seq"), None),
            P(("dp", "seq"), None, None),
        ),
        check_vma=False,
    )
```

```python
import functools

import jax
import jax.numpy as jnp
from jax import lax
from jax.experimental import pallas as pl
from jax.experimental.pallas import tpu as pltpu
from jax.sharding import PartitionSpec as P

HDIM = 128
P_SIZE = 512
F32 = jnp.float32
BF16 = jnp.bfloat16
LOW = -1e30


def dot_nt(a, b):
    return lax.dot_general(a, b, (((1,), (1,)), ((), ())), preferred_element_type=F32)


def dot_tn(a, b):
    return lax.dot_general(a, b, (((0,), (0,)), ((), ())), preferred_element_type=F32)


def dot_nn(a, b):
    return lax.dot_general(a, b, (((1,), (0,)), ((), ())), preferred_element_type=F32)


def flat(x):
    rows = 1
    for n in x.shape[:-1]:
        rows *= n
    if x.shape[-2] % 16:
        return x.astype(F32).reshape(rows, x.shape[-1]).astype(BF16)
    return x.reshape(rows, x.shape[-1])


def unflat(x, shape):
    if shape[-2] % 16:
        return x.reshape(shape).astype(BF16)
    return x.astype(BF16).reshape(shape)


def slopes(q, k, v, g, scale, bias):
    s = dot_nt(k, q) * scale
    if bias is not None:
        s = s + bias
    p = jnp.exp(s - jnp.max(s, axis=0, keepdims=True))
    w = p * (1.0 / jnp.sum(p, axis=0, keepdims=True))
    dp = dot_nt(v, g)
    delta = jnp.sum(w * dp, axis=0, keepdims=True)
    return w.astype(BF16), (w * (dp - delta)).astype(BF16)


def kernel(
    geo,
    live_ref, clen_ref, sqkv, tqkv, cq, cap_in, og,
    mixed, sgrad, tgrad, cqgrad, capgrad,
    srecv, sres, trecv, tres, crecv, cf, ckv, cbias, cacc, cg, cgu, cgd, fin, spo, tmo, wbuf, dbuf, tbias, cap, cap_rows, mix,
    loc, t_s, t_r, tb_s, tb_r, s_s, s_r, sb_s, sb_r, c1_s, c1_r, c2_s, c2_r, c3_s, c3_r, c4_s, c4_r,
):
    G, F, pix, W, HC, R, RP = geo
    S = G * F
    KP = S * RP
    T = F * pix
    scale = HDIM ** (-0.5)
    dev = lax.axis_index("seq")
    f = dev // G
    g = dev % G
    live = live_ref[0]
    clen = clen_ref[0]

    def cols(i):
        return pl.ds(pl.multiple_of(i * W, 128), W)

    def hcols(h):
        return pl.ds(pl.multiple_of(h * HDIM, 128), HDIM)

    def mate(o):
        return (g + o) % G

    def mate_from(o):
        return (g + G - o) % G

    def line(o):
        return (f + o) % F

    def line_from(o):
        return (f + F - o) % F

    def at_mate(i):
        return f * G + i

    def at_line(i):
        return i * G + g

    def remote(src, dst, ss, rs, to):
        return pltpu.make_async_remote_copy(
            src_ref=src, dst_ref=dst, send_sem=ss, recv_sem=rs,
            device_id={"seq": to}, device_id_type=pl.DeviceIdType.MESH,
        )

    cap_copy = pltpu.make_async_copy(cap_in, cap_rows, loc.at[0])
    cap_copy.start()
    barrier = pltpu.get_barrier_semaphore()
    for o in range(1, G):
        pl.semaphore_signal(barrier, inc=1, device_id={"seq": at_mate(mate(o))}, device_id_type=pl.DeviceIdType.MESH)
    for o in range(1, F):
        pl.semaphore_signal(barrier, inc=1, device_id={"seq": at_line(line(o))}, device_id_type=pl.DeviceIdType.MESH)

    local = [
        pltpu.make_async_copy(cap.at[:, :, cols(g)], crecv.at[dev], loc.at[0]),
        pltpu.make_async_copy(sqkv.at[:, :, :, cols(g)], srecv.at[pl.ds(0, 3), g], loc.at[1]),
        pltpu.make_async_copy(og.at[:, :, cols(g)], srecv.at[3, g], loc.at[2]),
        pltpu.make_async_copy(cq.at[:, :, cols(g)], srecv.at[4, g], loc.at[3]),
    ]
    for c in range(G):
        local.append(pltpu.make_async_copy(tqkv.at[:, f, :, cols(c)], trecv.at[c, pl.ds(0, 3), f], loc.at[4 + 2 * c]))
        local.append(pltpu.make_async_copy(og.at[f, :, cols(c)], trecv.at[c, 3, f], loc.at[5 + 2 * c]))
    cap_copy.wait()
    for i in range(2):
        cap[i] = cap_rows[:, i, :]
    pl.semaphore_wait(barrier, G + F - 2)

    def c1(o):
        return remote(cap.at[:, :, cols(mate(o))], crecv.at[dev], c1_s.at[o], c1_r.at[o], at_mate(mate(o)))

    def c1_in(o):
        i = mate_from(o)
        return remote(cap.at[:, :, cols(i)], crecv.at[at_mate(i)], c1_s.at[o], c1_r.at[o], at_mate(i))

    def t_out(c, o):
        j = line(o)
        return (
            remote(tqkv.at[:, j, :, cols(c)], trecv.at[c, pl.ds(0, 3), f], t_s.at[c, o, 0], t_r.at[c, o, 0], at_line(j)),
            remote(og.at[j, :, cols(c)], trecv.at[c, 3, f], t_s.at[c, o, 1], t_r.at[c, o, 1], at_line(j)),
        )

    def t_in(c, o):
        j = line_from(o)
        return (
            remote(tqkv.at[:, j, :, cols(c)], trecv.at[c, pl.ds(0, 3), j], t_s.at[c, o, 0], t_r.at[c, o, 0], at_line(j)),
            remote(og.at[j, :, cols(c)], trecv.at[c, 3, j], t_s.at[c, o, 1], t_r.at[c, o, 1], at_line(j)),
        )

    def s_out(o):
        i = mate(o)
        return (
            remote(sqkv.at[:, :, :, cols(i)], srecv.at[pl.ds(0, 3), g], s_s.at[o, 0], s_r.at[o, 0], at_mate(i)),
            remote(og.at[:, :, cols(i)], srecv.at[3, g], s_s.at[o, 1], s_r.at[o, 1], at_mate(i)),
            remote(cq.at[:, :, cols(i)], srecv.at[4, g], s_s.at[o, 2], s_r.at[o, 2], at_mate(i)),
        )

    def s_in(o):
        i = mate_from(o)
        return (
            remote(sqkv.at[:, :, :, cols(i)], srecv.at[pl.ds(0, 3), i], s_s.at[o, 0], s_r.at[o, 0], at_mate(i)),
            remote(og.at[:, :, cols(i)], srecv.at[3, i], s_s.at[o, 1], s_r.at[o, 1], at_mate(i)),
            remote(cq.at[:, :, cols(i)], srecv.at[4, i], s_s.at[o, 2], s_r.at[o, 2], at_mate(i)),
        )

    def send_chunk(c):
        for o in range(1, F):
            for copy in t_out(c, o):
                copy.start()

    for o in range(1, G):
        c1(o).start()
    send_chunk(0)
    for o in range(1, G):
        for copy in s_out(o):
            copy.start()

    def piece(i):
        return pl.ds(i * G, G)

    def up(i):
        return remote(crecv.at[piece(i)], crecv.at[piece(i)], c2_s.at[0, i], c2_r.at[0, i], at_line(line(1)))

    def down(i):
        return remote(crecv.at[piece(i)], crecv.at[piece(i)], c2_s.at[1, i], c2_r.at[1, i], at_line(line_from(1)))

    def gather_step(t):
        @pl.when(f >= t)
        def _():
            if t > 0:
                up(f - t).wait_recv()

            @pl.when(f < F - 1)
            def _():
                up(f - t).start()

        @pl.when(f + t < F)
        def _():
            if t > 0:
                down(f + t).wait_recv()

            @pl.when(f > 0)
            def _():
                down(f + t).start()

    for copy in local:
        copy.start()
    local[0].wait()
    for o in range(1, G):
        c1_in(o).wait_recv()
    gather_step(0)
    send_chunk(1)

    cf[...] = jnp.zeros(cf.shape, F32)
    cbias[...] = jnp.full(cbias.shape, LOW, F32)

    def live_rows(x, first):
        ids = first + lax.broadcasted_iota(jnp.int32, x.shape, 0)
        return jnp.where(ids < live, x.astype(F32), 0.0).astype(BF16)

    def many(k, v, q, gr, keys, bias):
        for b in range(G):
            rows = slice(b * T, (b + 1) * T)
            w, d = slopes(q[rows], k, v, gr[rows], scale, bias)
            wbuf[pl.ds(0, keys), rows] = w
            dbuf[pl.ds(0, keys), rows] = d
        w = wbuf[pl.ds(0, keys), :]
        d = dbuf[pl.ds(0, keys), :]
        return dot_tn(w, v), dot_tn(d, k) * scale, dot_nn(d, q) * scale, dot_nn(w, gr)

    rk = lax.broadcasted_iota(jnp.int32, (T, T), 0)
    rq = lax.broadcasted_iota(jnp.int32, (T, T), 1)
    shift = pix.bit_length() - 1
    first = g * T + f * pix
    key_token = (rk >> shift) * P_SIZE + (rk & (pix - 1)) + first
    same = ((rk & (pix - 1)) == (rq & (pix - 1))) & (key_token < live)
    tbias[...] = jnp.where(same, 0.0, LOW)

    def tb(c, o, j, src_j):
        return (
            remote(tres.at[c, 0, j], tmo.at[src_j, :, cols(c)], tb_s.at[c, o, 0], tb_r.at[c, o, 0], at_line(j)),
            remote(tres.at[c, pl.ds(1, 3), j], tgrad.at[:, src_j, :, cols(c)], tb_s.at[c, o, 1], tb_r.at[c, o, 1], at_line(j)),
        )

    tblock = (F, pix, HDIM)
    home = []

    def temporal_chunk(c):
        for o in range(1, F):
            for copy in t_in(c, o):
                copy.wait_recv()
        rd = lax.broadcasted_iota(jnp.int32, (T, HDIM), 0)
        t_live = ((rd >> shift) * P_SIZE + (rd & (pix - 1)) + first) < live
        for h in range(HC):
            at = pl.ds(h * HDIM, HDIM)
            q, k, v, gr = (flat(trecv[c, i, :, :, at]) for i in range(4))
            gr = jnp.where(t_live, gr.astype(F32), 0.0).astype(BF16)
            w, d = slopes(q, k, v, gr, scale, tbias[...])
            tres[c, 0, :, :, at] = unflat(dot_tn(w, v), tblock)
            tres[c, 1, :, :, at] = unflat(dot_tn(d, k) * scale, tblock)
            tres[c, 2, :, :, at] = unflat(dot_nn(d, q) * scale, tblock)
            tres[c, 3, :, :, at] = unflat(dot_nn(w, gr), tblock)
        for o in range(1, F):
            for copy in tb(c, o, line(o), f):
                copy.start()

    def temporal_home(c):
        mine = [
            pltpu.make_async_copy(tres.at[c, 0, f], tmo.at[f, :, cols(c)], loc.at[4 + 2 * c]),
            pltpu.make_async_copy(tres.at[c, pl.ds(1, 3), f], tgrad.at[:, f, :, cols(c)], loc.at[5 + 2 * c]),
        ]
        for copy in mine:
            copy.start()
        home.extend(mine)

    for c in range(G):
        local[4 + 2 * c].wait()
        local[5 + 2 * c].wait()
    for t in range(1, max(F - 1, 3)):
        if t <= 2:
            temporal_chunk(t - 1)
            temporal_home(t - 1)
        if t < F - 1:
            gather_step(t)
        if t + 1 < G:
            send_chunk(t + 1)
    for c in range(max(F - 1, 3) + 1, G):
        send_chunk(c)

    for copy in local[1:4]:
        copy.wait()
    for o in range(1, G):
        for copy in s_in(o):
            copy.wait_recv()

    block = (G, F, pix, HDIM)

    @pl.loop(0, HC)
    def _(h):
        at = hcols(h)
        q, k, v = (flat(srecv[i, :, :, :, at]) for i in range(3))
        gr = live_rows(flat(srecv[3, :, :, :, at]), f * (G * T))
        out, dq, dk, dv = many(k, v, q, gr, G * T, None)
        sres[0, :, :, :, at] = unflat(out, block)
        sres[1, :, :, :, at] = unflat(dq, block)
        sres[2, :, :, :, at] = unflat(dk, block)
        sres[3, :, :, :, at] = unflat(dv, block)

    def sb_grads(o, i, src_i):
        return remote(sres.at[pl.ds(1, 3), i], sgrad.at[:, :, :, cols(src_i)], sb_s.at[o, 0], sb_r.at[o, 0], at_mate(i))

    def sb_cross(o, i, src_i):
        return (
            remote(sres.at[0, i], spo.at[:, :, cols(src_i)], sb_s.at[o, 1], sb_r.at[o, 1], at_mate(i)),
            remote(sres.at[4, i], cqgrad.at[:, :, cols(src_i)], sb_s.at[o, 2], sb_r.at[o, 2], at_mate(i)),
        )

    for o in range(1, G):
        sb_grads(o, mate(o), g).start()
    home.append(pltpu.make_async_copy(sres.at[pl.ds(1, 3), g], sgrad.at[:, :, :, cols(g)], loc.at[0]))
    home[-1].start()

    @pl.when(f == F - 1)
    def _():
        up(0).wait_recv()

    @pl.when(f == 0)
    def _():
        down(F - 1).wait_recv()

    @pl.loop(0, S)
    def _(s):
        at = pl.ds(pl.multiple_of(s * RP, 8), R)
        for i in range(2):
            cf[i, at, :] = crecv[s, i].astype(F32)
        ids = s * R + lax.broadcasted_iota(jnp.int32, (R, HDIM), 0)
        cbias[at, :] = jnp.where(ids < clen, 0.0, LOW)

    ckv[...] = cf[...].astype(BF16)

    @pl.loop(0, HC)
    def _(h):
        at = hcols(h)
        q = flat(srecv[4, :, :, :, at])
        gr = live_rows(flat(srecv[3, :, :, :, at]), f * (G * T))
        k = ckv[0, :, at]
        v = ckv[1, :, at]
        out, dq, dk, dv = many(k, v, q, gr, KP, cbias[...])
        total = flat(sres[0, :, :, :, at]).astype(F32) + out
        sres[0, :, :, :, at] = unflat(total, block)
        sres[4, :, :, :, at] = unflat(dq, block)
        cacc[0, :, at] = dk
        cacc[1, :, at] = dv

    @pl.loop(0, S)
    def _(s):
        at = pl.ds(pl.multiple_of(s * RP, 8), R)
        for i in range(2):
            cg[s, i] = cacc[i, at, :].astype(BF16)

    def c3_up(j):
        return remote(cg.at[piece(j)], cgu.at[j], c3_s.at[0, j], c3_r.at[0, j], at_line(line(1)))

    def c3_down(j):
        return remote(cg.at[piece(j)], cgd.at[j], c3_s.at[1, j], c3_r.at[1, j], at_line(line_from(1)))

    def reduce_step(t):
        def hop(j, send, arrived):
            if t > 0:
                send.wait_recv()
                cg[piece(j)] = (cg[piece(j)].astype(F32) + arrived[j].astype(F32)).astype(BF16)
            send.start()

        @pl.when(f == t)
        def _():
            @pl.loop(0, F - 1 - t)
            def _(i):
                j = F - 1 - i
                hop(j, c3_up(j), cgu)

        @pl.when(f == F - 1 - t)
        def _():
            @pl.loop(0, F - 1 - t)
            def _(j):
                hop(j, c3_down(j), cgd)

    reduce_step(0)
    for o in range(1, G):
        for copy in sb_cross(o, mate(o), g):
            copy.start()
    home.append(pltpu.make_async_copy(sres.at[0, g], spo.at[:, :, cols(g)], loc.at[1]))
    home.append(pltpu.make_async_copy(sres.at[4, g], cqgrad.at[:, :, cols(g)], loc.at[2]))
    home[-2].start()
    home[-1].start()

    for t in range(1, max(F - 1, G - 1)):
        if t + 1 < G:
            temporal_chunk(t + 1)
            temporal_home(t + 1)
        if t < F - 1:
            reduce_step(t)

    for i in range(G):
        at = pl.ds(pl.multiple_of((f * G + i) * RP, 8), R)
        for b in range(2):
            fin[i, b] = cacc[b, at, :]

    @pl.when(f > 0)
    def _():
        c3_up(f).wait_recv()
        fin[...] += cgu[f].astype(F32)

    @pl.when(f < F - 1)
    def _():
        c3_down(f).wait_recv()
        fin[...] += cgd[f].astype(F32)

    def c4(o, i, src_i):
        return remote(fin.at[i], capgrad.at[:, :, cols(src_i)], c4_s.at[o], c4_r.at[o], at_mate(i))

    for o in range(1, G):
        c4(o, mate(o), g).start()
    home.append(pltpu.make_async_copy(fin.at[g], capgrad.at[:, :, cols(g)], loc.at[3]))
    home[-1].start()

    for o in range(1, G):
        i = mate_from(o)
        sb_grads(o, i, i).wait_recv()
        for copy in sb_cross(o, i, i):
            copy.wait_recv()
    for copy in home:
        copy.wait()

    @pl.loop(0, G)
    def _(c):
        for o in range(1, F):
            j = line_from(o)
            for copy in tb(c, o, j, j):
                copy.wait_recv()

    mixed_out = []
    shape3 = (F, pix, W)
    tok = (
        dev * T
        + lax.broadcasted_iota(jnp.int32, shape3, 0) * pix
        + lax.broadcasted_iota(jnp.int32, shape3, 1)
    )
    for c in range(G):
        at = slice(c * W, (c + 1) * W)
        total = spo[:, :, at].astype(F32) + tmo[:, :, at].astype(F32)
        mix[:, :, at] = jnp.where(tok < live, total, 0.0).astype(BF16)
        out = pltpu.make_async_copy(mix.at[:, :, pl.ds(c * W, W)], mixed.at[:, :, pl.ds(c * W, W)], loc.at[4 + 2 * c])
        out.start()
        mixed_out.append(out)

    for o in range(1, G):
        i = mate_from(o)
        c4(o, i, i).wait_recv()

    for copy in mixed_out:
        copy.wait()

    for o in range(1, G):
        c1(o).wait_send()
        for copy in s_out(o):
            copy.wait_send()
        sb_grads(o, mate(o), g).wait_send()
        for copy in sb_cross(o, mate(o), g):
            copy.wait_send()
        c4(o, mate(o), g).wait_send()

    @pl.when(f < F - 1)
    def _():
        @pl.loop(0, F)
        def _(i):
            @pl.when(i <= f)
            def _():
                up(i).wait_send()

            @pl.when(i > f)
            def _():
                c3_up(i).wait_send()

    @pl.when(f > 0)
    def _():
        @pl.loop(0, F)
        def _(i):
            @pl.when(i >= f)
            def _():
                down(i).wait_send()

            @pl.when(i < f)
            def _():
                c3_down(i).wait_send()

    @pl.loop(0, G)
    def _(c):
        for o in range(1, F):
            for copy in t_out(c, o):
                copy.wait_send()
            for copy in tb(c, o, line(o), f):
                copy.wait_send()


def hand_on(*refs):
    n = 4
    srcs, caps, dsts, capo = refs[:n], refs[n], refs[n + 1 : 2 * n + 1], refs[2 * n + 1]
    holds, (cap_in, cap_out, sem_in, sem_out) = refs[2 * n + 2 : 3 * n + 2], refs[3 * n + 2 :]
    pieces = []
    for src, hold, dst in zip(srcs, holds, dsts):
        if src.ndim == 3:
            pieces += [(src.at[i], hold.at[i], dst.at[i]) for i in range(src.shape[0])]
        else:
            half = src.shape[0] // 2
            pieces += [tuple(r.at[pl.ds(i * half, half)] for r in (src, hold, dst)) for i in range(2)]
    take = [pltpu.make_async_copy(a, b, sem_in.at[i]) for i, (a, b, _) in enumerate(pieces)]
    give = [pltpu.make_async_copy(b, c, sem_out.at[i]) for i, (_, b, c) in enumerate(pieces)]
    cap_take = pltpu.make_async_copy(caps, cap_in, sem_in.at[10])
    cap_take.start()
    for copy in take:
        copy.start()
    for first, second in zip(take, give):
        first.wait()
        second.start()
    cap_take.wait()
    for i in range(2):
        cap_out[:, i, :] = cap_in[i]
    give.append(pltpu.make_async_copy(cap_out, capo, sem_out.at[10]))
    give[-1].start()
    for copy in give:
        copy.wait()


def local(spatial_qkv, temporal_qkv, cross_query, caption_kv, out_grad, live_tokens, caption_len):
    devices = lax.axis_size("seq")
    rows, width = out_grad.shape
    G = P_SIZE // rows
    F = devices // G
    pix = rows // F
    W = width // G
    HC = W // HDIM
    R = caption_kv.shape[0]
    RP = (R + 7) // 8 * 8
    S = G * F
    KP = S * RP
    keys = max(KP, G * rows)
    geo = (G, F, pix, W, HC, R, RP)
    dma = pltpu.SemaphoreType.DMA
    any_spec = pl.BlockSpec(memory_space=pl.ANY)
    smem = pl.BlockSpec(memory_space=pltpu.SMEM)
    mixed, sgrad, tgrad, cqgrad, capgrad = pl.pallas_call(
        functools.partial(kernel, geo),
        out_shape=(
            jax.ShapeDtypeStruct((F, pix, width), BF16),
            jax.ShapeDtypeStruct((3, F, pix, width), BF16),
            jax.ShapeDtypeStruct((3, F, pix, width), BF16),
            jax.ShapeDtypeStruct((F, pix, width), BF16),
            jax.ShapeDtypeStruct((2, R, width), F32),
        ),
        in_specs=[smem, smem] + [any_spec] * 5,
        out_specs=(any_spec,) * 5,
        scratch_shapes=[
            pltpu.VMEM((5, G, F, pix, W), BF16),
            pltpu.VMEM((5, G, F, pix, W), BF16),
            pltpu.VMEM((G, 4, F, pix, W), BF16),
            pltpu.VMEM((G, 4, F, pix, W), BF16),
            pltpu.VMEM((S, 2, R, W), BF16),
            pltpu.VMEM((2, KP, W), F32),
            pltpu.VMEM((2, KP, W), BF16),
            pltpu.VMEM((KP, HDIM), F32),
            pltpu.VMEM((2, KP, W), F32),
            pltpu.VMEM((S, 2, R, W), BF16),
            pltpu.VMEM((F, G, 2, R, W), BF16),
            pltpu.VMEM((F, G, 2, R, W), BF16),
            pltpu.VMEM((G, 2, R, W), F32),
            pltpu.VMEM((F, pix, width), BF16),
            pltpu.VMEM((F, pix, width), BF16),
            pltpu.VMEM((keys, G * rows), BF16),
            pltpu.VMEM((keys, G * rows), BF16),
            pltpu.VMEM((rows, rows), F32),
            pltpu.VMEM((2, R, width), BF16),
            pltpu.VMEM((R, 2, width), BF16),
            pltpu.VMEM((F, pix, width), BF16),
            dma((4 + 2 * G,)),
            dma((G, F, 2)), dma((G, F, 2)),
            dma((G, F, 2)), dma((G, F, 2)),
            dma((G, 3)), dma((G, 3)),
            dma((G, 3)), dma((G, 3)),
            dma((G,)), dma((G,)),
            dma((2, F)), dma((2, F)),
            dma((2, F)), dma((2, F)),
            dma((G,)), dma((G,)),
        ],
        compiler_params=pltpu.CompilerParams(
            collective_id=0, has_side_effects=True, vmem_limit_bytes=60 * 1024 * 1024
        ),
    )(
        live_tokens,
        caption_len,
        spatial_qkv.reshape(3, F, pix, width),
        temporal_qkv.reshape(3, F, pix, width),
        cross_query.reshape(F, pix, width),
        caption_kv,
        out_grad.reshape(F, pix, width),
    )
    return pl.pallas_call(
        hand_on,
        out_shape=(
            jax.ShapeDtypeStruct((rows, width), BF16),
            jax.ShapeDtypeStruct((3, rows, width), BF16),
            jax.ShapeDtypeStruct((3, rows, width), BF16),
            jax.ShapeDtypeStruct((rows, width), BF16),
            jax.ShapeDtypeStruct((R, 2, width), F32),
        ),
        in_specs=[any_spec] * 5,
        out_specs=(any_spec,) * 5,
        scratch_shapes=[
            pltpu.VMEM((rows, width), BF16),
            pltpu.VMEM((3, rows, width), BF16),
            pltpu.VMEM((3, rows, width), BF16),
            pltpu.VMEM((rows, width), BF16),
            pltpu.VMEM((2, R, width), F32),
            pltpu.VMEM((R, 2, width), F32),
            dma((11,)),
            dma((11,)),
        ],
        compiler_params=pltpu.CompilerParams(vmem_limit_bytes=60 * 1024 * 1024),
    )(
        mixed.reshape(rows, width),
        sgrad.reshape(3, rows, width),
        tgrad.reshape(3, rows, width),
        cqgrad.reshape(rows, width),
        capgrad,
    )


def solution(mesh):
    placed = (
        P(None, ("dp", "seq"), None),
        P(None, ("dp", "seq"), None),
        P(("dp", "seq"), None),
        P(("dp", "seq"), None, None),
        P(("dp", "seq"), None),
        P("dp"),
        P("dp"),
    )
    return jax.shard_map(
        local,
        mesh=mesh,
        in_specs=placed,
        out_specs=(
            P(("dp", "seq"), None),
            P(None, ("dp", "seq"), None),
            P(None, ("dp", "seq"), None),
            P(("dp", "seq"), None),
            P(("dp", "seq"), None, None),
        ),
        check_vma=False,
    )
```

```python
import functools

import jax
import jax.numpy as jnp
from jax import lax
from jax.experimental import pallas as pl
from jax.experimental.pallas import tpu as pltpu
from jax.sharding import PartitionSpec as P

HDIM = 128
P_SIZE = 512
F32 = jnp.float32
BF16 = jnp.bfloat16
LOW = -1e30


def dot_nt(a, b):
    return lax.dot_general(a, b, (((1,), (1,)), ((), ())), preferred_element_type=F32)


def dot_tn(a, b):
    return lax.dot_general(a, b, (((0,), (0,)), ((), ())), preferred_element_type=F32)


def dot_nn(a, b):
    return lax.dot_general(a, b, (((1,), (0,)), ((), ())), preferred_element_type=F32)


def flat(x):
    rows = 1
    for n in x.shape[:-1]:
        rows *= n
    if x.shape[-2] % 16:
        return x.astype(F32).reshape(rows, x.shape[-1]).astype(BF16)
    return x.reshape(rows, x.shape[-1])


def unflat(x, shape):
    if shape[-2] % 16:
        return x.reshape(shape).astype(BF16)
    return x.astype(BF16).reshape(shape)


def slopes(q, k, v, g, scale, bias):
    s = dot_nt(k, q) * scale
    if bias is not None:
        s = s + bias
    p = jnp.exp(s - jnp.max(s, axis=0, keepdims=True))
    w = p * (1.0 / jnp.sum(p, axis=0, keepdims=True))
    dp = dot_nt(v, g)
    delta = jnp.sum(w * dp, axis=0, keepdims=True)
    return w.astype(BF16), (w * (dp - delta)).astype(BF16)


def kernel(
    geo,
    live_ref, clen_ref, sqkv, tqkv, cq, cap_in, og,
    mixed, sgrad, tgrad, cqgrad, capgrad,
    srecv, sres, trecv, tres, crecv, cf, ckv, cbias, cacc, cg, cgu, cgd, fin, spo, tmo, wbuf, dbuf, tbias, cap, cap_rows, mix,
    loc, t_s, t_r, tb_s, tb_r, s_s, s_r, sb_s, sb_r, c1_s, c1_r, c2_s, c2_r, c3_s, c3_r, c4_s, c4_r,
):
    G, F, pix, W, HC, R, RP = geo
    S = G * F
    KP = S * RP
    T = F * pix
    scale = HDIM ** (-0.5)
    dev = lax.axis_index("seq")
    f = dev // G
    g = dev % G
    live = live_ref[0]
    clen = clen_ref[0]

    def cols(i):
        return pl.ds(pl.multiple_of(i * W, 128), W)

    def hcols(h):
        return pl.ds(pl.multiple_of(h * HDIM, 128), HDIM)

    def mate(o):
        return (g + o) % G

    def mate_from(o):
        return (g + G - o) % G

    def line(o):
        return (f + o) % F

    def line_from(o):
        return (f + F - o) % F

    def at_mate(i):
        return f * G + i

    def at_line(i):
        return i * G + g

    def remote(src, dst, ss, rs, to):
        return pltpu.make_async_remote_copy(
            src_ref=src, dst_ref=dst, send_sem=ss, recv_sem=rs,
            device_id={"seq": to}, device_id_type=pl.DeviceIdType.MESH,
        )

    cap_copy = pltpu.make_async_copy(cap_in, cap_rows, loc.at[0])
    cap_copy.start()
    barrier = pltpu.get_barrier_semaphore()
    for o in range(1, G):
        pl.semaphore_signal(barrier, inc=1, device_id={"seq": at_mate(mate(o))}, device_id_type=pl.DeviceIdType.MESH)
    for o in range(1, F):
        pl.semaphore_signal(barrier, inc=1, device_id={"seq": at_line(line(o))}, device_id_type=pl.DeviceIdType.MESH)

    local = [
        pltpu.make_async_copy(cap.at[:, :, cols(g)], crecv.at[dev], loc.at[0]),
        pltpu.make_async_copy(sqkv.at[:, :, :, cols(g)], srecv.at[pl.ds(0, 3), g], loc.at[1]),
        pltpu.make_async_copy(og.at[:, :, cols(g)], srecv.at[3, g], loc.at[2]),
        pltpu.make_async_copy(cq.at[:, :, cols(g)], srecv.at[4, g], loc.at[3]),
    ]
    for c in range(G):
        local.append(pltpu.make_async_copy(tqkv.at[:, f, :, cols(c)], trecv.at[c, pl.ds(0, 3), f], loc.at[4 + 2 * c]))
        local.append(pltpu.make_async_copy(og.at[f, :, cols(c)], trecv.at[c, 3, f], loc.at[5 + 2 * c]))
    cap_copy.wait()
    for i in range(2):
        cap[i] = cap_rows[:, i, :]
    pl.semaphore_wait(barrier, G + F - 2)

    def c1(o):
        return remote(cap.at[:, :, cols(mate(o))], crecv.at[dev], c1_s.at[o], c1_r.at[o], at_mate(mate(o)))

    def c1_in(o):
        i = mate_from(o)
        return remote(cap.at[:, :, cols(i)], crecv.at[at_mate(i)], c1_s.at[o], c1_r.at[o], at_mate(i))

    def t_out(c, o):
        j = line(o)
        return (
            remote(tqkv.at[:, j, :, cols(c)], trecv.at[c, pl.ds(0, 3), f], t_s.at[c, o, 0], t_r.at[c, o, 0], at_line(j)),
            remote(og.at[j, :, cols(c)], trecv.at[c, 3, f], t_s.at[c, o, 1], t_r.at[c, o, 1], at_line(j)),
        )

    def t_in(c, o):
        j = line_from(o)
        return (
            remote(tqkv.at[:, j, :, cols(c)], trecv.at[c, pl.ds(0, 3), j], t_s.at[c, o, 0], t_r.at[c, o, 0], at_line(j)),
            remote(og.at[j, :, cols(c)], trecv.at[c, 3, j], t_s.at[c, o, 1], t_r.at[c, o, 1], at_line(j)),
        )

    def s_out(o):
        i = mate(o)
        return (
            remote(sqkv.at[:, :, :, cols(i)], srecv.at[pl.ds(0, 3), g], s_s.at[o, 0], s_r.at[o, 0], at_mate(i)),
            remote(og.at[:, :, cols(i)], srecv.at[3, g], s_s.at[o, 1], s_r.at[o, 1], at_mate(i)),
            remote(cq.at[:, :, cols(i)], srecv.at[4, g], s_s.at[o, 2], s_r.at[o, 2], at_mate(i)),
        )

    def s_in(o):
        i = mate_from(o)
        return (
            remote(sqkv.at[:, :, :, cols(i)], srecv.at[pl.ds(0, 3), i], s_s.at[o, 0], s_r.at[o, 0], at_mate(i)),
            remote(og.at[:, :, cols(i)], srecv.at[3, i], s_s.at[o, 1], s_r.at[o, 1], at_mate(i)),
            remote(cq.at[:, :, cols(i)], srecv.at[4, i], s_s.at[o, 2], s_r.at[o, 2], at_mate(i)),
        )

    def send_chunk(c):
        for o in range(1, F):
            for copy in t_out(c, o):
                copy.start()

    for o in range(1, G):
        c1(o).start()
    send_chunk(0)
    for o in range(1, G):
        for copy in s_out(o):
            copy.start()

    def piece(i):
        return pl.ds(i * G, G)

    def up(i):
        return remote(crecv.at[piece(i)], crecv.at[piece(i)], c2_s.at[0, i], c2_r.at[0, i], at_line(line(1)))

    def down(i):
        return remote(crecv.at[piece(i)], crecv.at[piece(i)], c2_s.at[1, i], c2_r.at[1, i], at_line(line_from(1)))

    def gather_step(t):
        @pl.when(f >= t)
        def _():
            if t > 0:
                up(f - t).wait_recv()

            @pl.when(f < F - 1)
            def _():
                up(f - t).start()

        @pl.when(f + t < F)
        def _():
            if t > 0:
                down(f + t).wait_recv()

            @pl.when(f > 0)
            def _():
                down(f + t).start()

    send_chunk(1)
    for copy in local:
        copy.start()
    local[0].wait()
    for o in range(1, G):
        c1_in(o).wait_recv()
    gather_step(0)

    cf[...] = jnp.zeros(cf.shape, F32)
    cbias[...] = jnp.full(cbias.shape, LOW, F32)

    def live_rows(x, first):
        ids = first + lax.broadcasted_iota(jnp.int32, x.shape, 0)
        return jnp.where(ids < live, x.astype(F32), 0.0).astype(BF16)

    def many(k, v, q, gr, keys, bias):
        for b in range(G):
            rows = slice(b * T, (b + 1) * T)
            w, d = slopes(q[rows], k, v, gr[rows], scale, bias)
            wbuf[pl.ds(0, keys), rows] = w
            dbuf[pl.ds(0, keys), rows] = d
        w = wbuf[pl.ds(0, keys), :]
        d = dbuf[pl.ds(0, keys), :]
        return dot_tn(w, v), dot_tn(d, k) * scale, dot_nn(d, q) * scale, dot_nn(w, gr)

    rk = lax.broadcasted_iota(jnp.int32, (T, T), 0)
    rq = lax.broadcasted_iota(jnp.int32, (T, T), 1)
    shift = pix.bit_length() - 1
    first = g * T + f * pix
    key_token = (rk >> shift) * P_SIZE + (rk & (pix - 1)) + first
    same = ((rk & (pix - 1)) == (rq & (pix - 1))) & (key_token < live)
    tbias[...] = jnp.where(same, 0.0, LOW)

    def tb(c, o, j, src_j):
        return (
            remote(tres.at[c, 0, j], tmo.at[src_j, :, cols(c)], tb_s.at[c, o, 0], tb_r.at[c, o, 0], at_line(j)),
            remote(tres.at[c, pl.ds(1, 3), j], tgrad.at[:, src_j, :, cols(c)], tb_s.at[c, o, 1], tb_r.at[c, o, 1], at_line(j)),
        )

    tblock = (F, pix, HDIM)
    home = []

    def temporal_chunk(c):
        for o in range(1, F):
            for copy in t_in(c, o):
                copy.wait_recv()
        rd = lax.broadcasted_iota(jnp.int32, (T, HDIM), 0)
        t_live = ((rd >> shift) * P_SIZE + (rd & (pix - 1)) + first) < live
        for h in range(HC):
            at = pl.ds(h * HDIM, HDIM)
            q, k, v, gr = (flat(trecv[c, i, :, :, at]) for i in range(4))
            gr = jnp.where(t_live, gr.astype(F32), 0.0).astype(BF16)
            w, d = slopes(q, k, v, gr, scale, tbias[...])
            tres[c, 0, :, :, at] = unflat(dot_tn(w, v), tblock)
            tres[c, 1, :, :, at] = unflat(dot_tn(d, k) * scale, tblock)
            tres[c, 2, :, :, at] = unflat(dot_nn(d, q) * scale, tblock)
            tres[c, 3, :, :, at] = unflat(dot_nn(w, gr), tblock)
        for o in range(1, F):
            for copy in tb(c, o, line(o), f):
                copy.start()

    def temporal_home(c):
        mine = [
            pltpu.make_async_copy(tres.at[c, 0, f], tmo.at[f, :, cols(c)], loc.at[4 + 2 * c]),
            pltpu.make_async_copy(tres.at[c, pl.ds(1, 3), f], tgrad.at[:, f, :, cols(c)], loc.at[5 + 2 * c]),
        ]
        for copy in mine:
            copy.start()
        home.extend(mine)

    for c in range(G):
        local[4 + 2 * c].wait()
        local[5 + 2 * c].wait()
    for t in range(1, max(F - 1, 3)):
        if t <= 2:
            temporal_chunk(t - 1)
            temporal_home(t - 1)
        if t < F - 1:
            gather_step(t)
        if t + 1 < G:
            send_chunk(t + 1)
    for c in range(max(F - 1, 3) + 1, G):
        send_chunk(c)

    for copy in local[1:4]:
        copy.wait()
    for o in range(1, G):
        for copy in s_in(o):
            copy.wait_recv()

    block = (G, F, pix, HDIM)

    @pl.loop(0, HC)
    def _(h):
        at = hcols(h)
        q, k, v = (flat(srecv[i, :, :, :, at]) for i in range(3))
        gr = live_rows(flat(srecv[3, :, :, :, at]), f * (G * T))
        out, dq, dk, dv = many(k, v, q, gr, G * T, None)
        sres[0, :, :, :, at] = unflat(out, block)
        sres[1, :, :, :, at] = unflat(dq, block)
        sres[2, :, :, :, at] = unflat(dk, block)
        sres[3, :, :, :, at] = unflat(dv, block)

    def sb_grads(o, i, src_i):
        return remote(sres.at[pl.ds(1, 3), i], sgrad.at[:, :, :, cols(src_i)], sb_s.at[o, 0], sb_r.at[o, 0], at_mate(i))

    def sb_cross(o, i, src_i):
        return (
            remote(sres.at[0, i], spo.at[:, :, cols(src_i)], sb_s.at[o, 1], sb_r.at[o, 1], at_mate(i)),
            remote(sres.at[4, i], cqgrad.at[:, :, cols(src_i)], sb_s.at[o, 2], sb_r.at[o, 2], at_mate(i)),
        )

    for o in range(1, G):
        sb_grads(o, mate(o), g).start()
    home.append(pltpu.make_async_copy(sres.at[pl.ds(1, 3), g], sgrad.at[:, :, :, cols(g)], loc.at[0]))
    home[-1].start()

    @pl.when(f == F - 1)
    def _():
        up(0).wait_recv()

    @pl.when(f == 0)
    def _():
        down(F - 1).wait_recv()

    @pl.loop(0, S)
    def _(s):
        at = pl.ds(pl.multiple_of(s * RP, 8), R)
        for i in range(2):
            cf[i, at, :] = crecv[s, i].astype(F32)
        ids = s * R + lax.broadcasted_iota(jnp.int32, (R, HDIM), 0)
        cbias[at, :] = jnp.where(ids < clen, 0.0, LOW)

    ckv[...] = cf[...].astype(BF16)

    @pl.loop(0, HC)
    def _(h):
        at = hcols(h)
        q = flat(srecv[4, :, :, :, at])
        gr = live_rows(flat(srecv[3, :, :, :, at]), f * (G * T))
        k = ckv[0, :, at]
        v = ckv[1, :, at]
        out, dq, dk, dv = many(k, v, q, gr, KP, cbias[...])
        total = flat(sres[0, :, :, :, at]).astype(F32) + out
        sres[0, :, :, :, at] = unflat(total, block)
        sres[4, :, :, :, at] = unflat(dq, block)
        cacc[0, :, at] = dk
        cacc[1, :, at] = dv

    @pl.loop(0, S)
    def _(s):
        at = pl.ds(pl.multiple_of(s * RP, 8), R)
        for i in range(2):
            cg[s, i] = cacc[i, at, :].astype(BF16)

    def c3_up(j):
        return remote(cg.at[piece(j)], cgu.at[j], c3_s.at[0, j], c3_r.at[0, j], at_line(line(1)))

    def c3_down(j):
        return remote(cg.at[piece(j)], cgd.at[j], c3_s.at[1, j], c3_r.at[1, j], at_line(line_from(1)))

    def reduce_step(t):
        def hop(j, send, arrived):
            if t > 0:
                send.wait_recv()
                cg[piece(j)] = (cg[piece(j)].astype(F32) + arrived[j].astype(F32)).astype(BF16)
            send.start()

        @pl.when(f == t)
        def _():
            @pl.loop(0, F - 1 - t)
            def _(i):
                j = F - 1 - i
                hop(j, c3_up(j), cgu)

        @pl.when(f == F - 1 - t)
        def _():
            @pl.loop(0, F - 1 - t)
            def _(j):
                hop(j, c3_down(j), cgd)

    reduce_step(0)
    for o in range(1, G):
        for copy in sb_cross(o, mate(o), g):
            copy.start()
    home.append(pltpu.make_async_copy(sres.at[0, g], spo.at[:, :, cols(g)], loc.at[1]))
    home.append(pltpu.make_async_copy(sres.at[4, g], cqgrad.at[:, :, cols(g)], loc.at[2]))
    home[-2].start()
    home[-1].start()

    for t in range(1, max(F - 1, G - 1)):
        if t + 1 < G:
            temporal_chunk(t + 1)
            temporal_home(t + 1)
        if t < F - 1:
            reduce_step(t)

    for i in range(G):
        at = pl.ds(pl.multiple_of((f * G + i) * RP, 8), R)
        for b in range(2):
            fin[i, b] = cacc[b, at, :]

    @pl.when(f > 0)
    def _():
        c3_up(f).wait_recv()
        fin[...] += cgu[f].astype(F32)

    @pl.when(f < F - 1)
    def _():
        c3_down(f).wait_recv()
        fin[...] += cgd[f].astype(F32)

    def c4(o, i, src_i):
        return remote(fin.at[i], capgrad.at[:, :, cols(src_i)], c4_s.at[o], c4_r.at[o], at_mate(i))

    for o in range(1, G):
        c4(o, mate(o), g).start()
    home.append(pltpu.make_async_copy(fin.at[g], capgrad.at[:, :, cols(g)], loc.at[3]))
    home[-1].start()

    for o in range(1, G):
        i = mate_from(o)
        sb_grads(o, i, i).wait_recv()
        for copy in sb_cross(o, i, i):
            copy.wait_recv()
    for copy in home:
        copy.wait()

    @pl.loop(0, G)
    def _(c):
        for o in range(1, F):
            j = line_from(o)
            for copy in tb(c, o, j, j):
                copy.wait_recv()

    mixed_out = []
    shape3 = (F, pix, W)
    tok = (
        dev * T
        + lax.broadcasted_iota(jnp.int32, shape3, 0) * pix
        + lax.broadcasted_iota(jnp.int32, shape3, 1)
    )
    for c in range(G):
        at = slice(c * W, (c + 1) * W)
        total = spo[:, :, at].astype(F32) + tmo[:, :, at].astype(F32)
        mix[:, :, at] = jnp.where(tok < live, total, 0.0).astype(BF16)
        out = pltpu.make_async_copy(mix.at[:, :, pl.ds(c * W, W)], mixed.at[:, :, pl.ds(c * W, W)], loc.at[4 + 2 * c])
        out.start()
        mixed_out.append(out)

    for o in range(1, G):
        i = mate_from(o)
        c4(o, i, i).wait_recv()

    for copy in mixed_out:
        copy.wait()

    for o in range(1, G):
        c1(o).wait_send()
        for copy in s_out(o):
            copy.wait_send()
        sb_grads(o, mate(o), g).wait_send()
        for copy in sb_cross(o, mate(o), g):
            copy.wait_send()
        c4(o, mate(o), g).wait_send()

    @pl.when(f < F - 1)
    def _():
        @pl.loop(0, F)
        def _(i):
            @pl.when(i <= f)
            def _():
                up(i).wait_send()

            @pl.when(i > f)
            def _():
                c3_up(i).wait_send()

    @pl.when(f > 0)
    def _():
        @pl.loop(0, F)
        def _(i):
            @pl.when(i >= f)
            def _():
                down(i).wait_send()

            @pl.when(i < f)
            def _():
                c3_down(i).wait_send()

    @pl.loop(0, G)
    def _(c):
        for o in range(1, F):
            for copy in t_out(c, o):
                copy.wait_send()
            for copy in tb(c, o, line(o), f):
                copy.wait_send()


def hand_on(*refs):
    n = 4
    srcs, caps, dsts, capo = refs[:n], refs[n], refs[n + 1 : 2 * n + 1], refs[2 * n + 1]
    holds, (cap_in, cap_out, sem_in, sem_out) = refs[2 * n + 2 : 3 * n + 2], refs[3 * n + 2 :]
    pieces = []
    for src, hold, dst in zip(srcs, holds, dsts):
        if src.ndim == 3:
            pieces += [(src.at[i], hold.at[i], dst.at[i]) for i in range(src.shape[0])]
        else:
            half = src.shape[0] // 2
            pieces += [tuple(r.at[pl.ds(i * half, half)] for r in (src, hold, dst)) for i in range(2)]
    take = [pltpu.make_async_copy(a, b, sem_in.at[i]) for i, (a, b, _) in enumerate(pieces)]
    give = [pltpu.make_async_copy(b, c, sem_out.at[i]) for i, (_, b, c) in enumerate(pieces)]
    cap_take = pltpu.make_async_copy(caps, cap_in, sem_in.at[10])
    cap_take.start()
    for copy in take:
        copy.start()
    for first, second in zip(take, give):
        first.wait()
        second.start()
    cap_take.wait()
    for i in range(2):
        cap_out[:, i, :] = cap_in[i]
    give.append(pltpu.make_async_copy(cap_out, capo, sem_out.at[10]))
    give[-1].start()
    for copy in give:
        copy.wait()


def local(spatial_qkv, temporal_qkv, cross_query, caption_kv, out_grad, live_tokens, caption_len):
    devices = lax.axis_size("seq")
    rows, width = out_grad.shape
    G = P_SIZE // rows
    F = devices // G
    pix = rows // F
    W = width // G
    HC = W // HDIM
    R = caption_kv.shape[0]
    RP = (R + 7) // 8 * 8
    S = G * F
    KP = S * RP
    keys = max(KP, G * rows)
    geo = (G, F, pix, W, HC, R, RP)
    dma = pltpu.SemaphoreType.DMA
    any_spec = pl.BlockSpec(memory_space=pl.ANY)
    smem = pl.BlockSpec(memory_space=pltpu.SMEM)
    mixed, sgrad, tgrad, cqgrad, capgrad = pl.pallas_call(
        functools.partial(kernel, geo),
        out_shape=(
            jax.ShapeDtypeStruct((F, pix, width), BF16),
            jax.ShapeDtypeStruct((3, F, pix, width), BF16),
            jax.ShapeDtypeStruct((3, F, pix, width), BF16),
            jax.ShapeDtypeStruct((F, pix, width), BF16),
            jax.ShapeDtypeStruct((2, R, width), F32),
        ),
        in_specs=[smem, smem] + [any_spec] * 5,
        out_specs=(any_spec,) * 5,
        scratch_shapes=[
            pltpu.VMEM((5, G, F, pix, W), BF16),
            pltpu.VMEM((5, G, F, pix, W), BF16),
            pltpu.VMEM((G, 4, F, pix, W), BF16),
            pltpu.VMEM((G, 4, F, pix, W), BF16),
            pltpu.VMEM((S, 2, R, W), BF16),
            pltpu.VMEM((2, KP, W), F32),
            pltpu.VMEM((2, KP, W), BF16),
            pltpu.VMEM((KP, HDIM), F32),
            pltpu.VMEM((2, KP, W), F32),
            pltpu.VMEM((S, 2, R, W), BF16),
            pltpu.VMEM((F, G, 2, R, W), BF16),
            pltpu.VMEM((F, G, 2, R, W), BF16),
            pltpu.VMEM((G, 2, R, W), F32),
            pltpu.VMEM((F, pix, width), BF16),
            pltpu.VMEM((F, pix, width), BF16),
            pltpu.VMEM((keys, G * rows), BF16),
            pltpu.VMEM((keys, G * rows), BF16),
            pltpu.VMEM((rows, rows), F32),
            pltpu.VMEM((2, R, width), BF16),
            pltpu.VMEM((R, 2, width), BF16),
            pltpu.VMEM((F, pix, width), BF16),
            dma((4 + 2 * G,)),
            dma((G, F, 2)), dma((G, F, 2)),
            dma((G, F, 2)), dma((G, F, 2)),
            dma((G, 3)), dma((G, 3)),
            dma((G, 3)), dma((G, 3)),
            dma((G,)), dma((G,)),
            dma((2, F)), dma((2, F)),
            dma((2, F)), dma((2, F)),
            dma((G,)), dma((G,)),
        ],
        compiler_params=pltpu.CompilerParams(
            collective_id=0, has_side_effects=True, vmem_limit_bytes=60 * 1024 * 1024
        ),
    )(
        live_tokens,
        caption_len,
        spatial_qkv.reshape(3, F, pix, width),
        temporal_qkv.reshape(3, F, pix, width),
        cross_query.reshape(F, pix, width),
        caption_kv,
        out_grad.reshape(F, pix, width),
    )
    return pl.pallas_call(
        hand_on,
        out_shape=(
            jax.ShapeDtypeStruct((rows, width), BF16),
            jax.ShapeDtypeStruct((3, rows, width), BF16),
            jax.ShapeDtypeStruct((3, rows, width), BF16),
            jax.ShapeDtypeStruct((rows, width), BF16),
            jax.ShapeDtypeStruct((R, 2, width), F32),
        ),
        in_specs=[any_spec] * 5,
        out_specs=(any_spec,) * 5,
        scratch_shapes=[
            pltpu.VMEM((rows, width), BF16),
            pltpu.VMEM((3, rows, width), BF16),
            pltpu.VMEM((3, rows, width), BF16),
            pltpu.VMEM((rows, width), BF16),
            pltpu.VMEM((2, R, width), F32),
            pltpu.VMEM((R, 2, width), F32),
            dma((11,)),
            dma((11,)),
        ],
        compiler_params=pltpu.CompilerParams(vmem_limit_bytes=60 * 1024 * 1024),
    )(
        mixed.reshape(rows, width),
        sgrad.reshape(3, rows, width),
        tgrad.reshape(3, rows, width),
        cqgrad.reshape(rows, width),
        capgrad,
    )


def solution(mesh):
    placed = (
        P(None, ("dp", "seq"), None),
        P(None, ("dp", "seq"), None),
        P(("dp", "seq"), None),
        P(("dp", "seq"), None, None),
        P(("dp", "seq"), None),
        P("dp"),
        P("dp"),
    )
    return jax.shard_map(
        local,
        mesh=mesh,
        in_specs=placed,
        out_specs=(
            P(("dp", "seq"), None),
            P(None, ("dp", "seq"), None),
            P(None, ("dp", "seq"), None),
            P(("dp", "seq"), None),
            P(("dp", "seq"), None, None),
        ),
        check_vma=False,
    )
```
